128 devices in a mesh: img: 16 (over y, z_lo, core), patch: 8 (over z_hi, x).
Axes of the slice: x: 4, y: 4, z: 4 (z_hi: 2, z_lo: 2; z = z_hi * 2 + z_lo), core: 2. Of those that a mesh axis runs over, the one named last changes fastest.
Arguments:
- latents_now: bfloat16 [16, 2048, 1280], P('img', 'patch'), may hold values from -6 to 6
- latents_stale: bfloat16 [16, 2048, 1280], P('img', 'patch'), may hold values from -6 to 6
- w_query: bfloat16 [1280, 640], replicated, may hold values from -1 to 1
- w_key: bfloat16 [1280, 640], replicated, may hold values from -1 to 1
- w_value: bfloat16 [1280, 640], replicated, may hold values from -0.15625 to 0.15625
- w_out: bfloat16 [640, 1280], replicated, may hold values from -1.5 to 1.5
- cotangent: bfloat16 [16, 2048, 1280], P('img', 'patch'), may hold values from -6 to 6
Outputs:
- mixed: bfloat16 [16, 2048, 1280], P('img', 'patch')
- grad_latents: bfloat16 [16, 2048, 1280], P('img', 'patch')
- grad_value: float32 [1280, 640], P('patch')
- grad_out: float32 [640, 1280], P('patch')
The draws below stay inside these ranges and needn't reach their ends.
All inputs are finite; a program needn't handle non-finite values.
Results may differ from the reference program's by a relative error of at most 0.029.
Values may be sent and summed in bfloat16 or wider, within the bound.
A program may use at most 192 MiB of HBM per device.

```python
import jax
import jax.numpy as jnp
from jax import lax

C = 1280
HEADS = 10
HEAD_DIM = 64
TOK_DEV = 256
INNER = 640
TOKENS = 2048
IMAGES = 16
N_PATCH = 8


def shared_normal(key):
    return jnp.clip(jax.random.normal(key, (C, INNER), jnp.float32), -5.0, 5.0)


def draw_w_query(key, part):
    common = shared_normal(key)
    return (common * C ** (-0.5)).astype(jnp.bfloat16)


def draw_w_key(key, part):
    key = jax.random.fold_in(key, 12)
    own_part = jnp.clip(jax.random.normal(key, (C, INNER), jnp.float32), -5.0, 5.0)
    return (own_part * C ** (-0.5)).astype(jnp.bfloat16)


def draw_latents_now(key, part):
    key = jax.random.fold_in(key, 13)
    base_key = jax.random.fold_in(key, 0)
    latent = jnp.clip(jax.random.normal(base_key, (IMAGES, TOKENS, C), jnp.float32), -6.0, 6.0)
    return latent.astype(jnp.bfloat16)


def block_scale(key, extent, pieces, smallest, largest):
    level, own = 1.0, jax.random.fold_in(key, 6)
    for axis_at, shards_of in pieces:
        draws = jnp.exp(jax.random.uniform(jax.random.fold_in(own, axis_at), (shards_of,), jnp.float32, smallest / len(pieces), largest / len(pieces)))
        level = level * jnp.repeat(draws, extent[axis_at] // shards_of).reshape([-1 if axis == axis_at else 1 for axis in range(len(extent))])
    return level


def bell_draw(own_key, shape, deviation, bound, cuts=(), kind=jnp.bfloat16):
    loudness = block_scale(own_key, shape, cuts, -0.22, 0.18) if cuts else 1.0
    drawn = jax.random.normal(own_key, shape, jnp.float32) * deviation * loudness
    return jnp.minimum(jnp.maximum(drawn, -bound), bound).astype(kind)


def setup_inputs(seed: int = 0) -> dict:
    keys = jax.random.split(jax.random.key(seed), 8)
    latents_now = draw_latents_now(jax.random.fold_in(keys[7], 71), 0)
    latents_stale = bell_draw(keys[1], (IMAGES, TOKENS, C), 1.0, 6.0, ((0, 16), (1, 8)))
    w_query = draw_w_query(jax.random.fold_in(keys[7], 71), 0)
    w_key = draw_w_key(jax.random.fold_in(keys[7], 71), 0)
    w_value = bell_draw(keys[4], (C, INNER), C ** -0.5, 0.15625)
    w_out = bell_draw(keys[5], (INNER, C), 16 ** -0.5, 1.5)
    cotangent = bell_draw(keys[6], (IMAGES, TOKENS, C), 1.0, 6.0, ((0, 16), (1, 8)))
    return dict(latents_now=latents_now, latents_stale=latents_stale, w_query=w_query, w_key=w_key, w_value=w_value, w_out=w_out, cotangent=cotangent)


def project(a, w):
    return jnp.dot(a, w, preferred_element_type=jnp.float32).astype(jnp.bfloat16)


def split_heads(a):
    return a.reshape(a.shape[0], HEADS, HEAD_DIM).astype(jnp.float32)


def reference(latents_now, latents_stale, w_query, w_key, w_value, w_out, cotangent):
    scale = HEAD_DIM ** -0.5

    def one_image(pack):
        x, stale, g = pack
        q = split_heads(project(x, w_query))
        k = split_heads(project(x, w_key))
        v = split_heads(project(x, w_value))
        k_old = split_heads(project(stale, w_key))
        v_old = split_heads(project(stale, w_value))
        block = jnp.arange(TOKENS) // TOK_DEV
        same = (block[:, None] == block[None, :])[None]
        fresh = jnp.einsum("qhd,khd->hqk", q, k) * scale
        older = jnp.einsum("qhd,khd->hqk", q, k_old) * scale
        scores = jnp.where(same, fresh, older)
        weights = jax.nn.softmax(scores, axis=-1).astype(jnp.bfloat16).astype(jnp.float32)
        att = jnp.einsum("hqk,khd->qhd", jnp.where(same, weights, 0.0), v)
        att = att + jnp.einsum("hqk,khd->qhd", jnp.where(same, 0.0, weights), v_old)
        att = att.reshape(TOKENS, INNER).astype(jnp.bfloat16)
        mixed = jnp.dot(att, w_out, preferred_element_type=jnp.float32).astype(jnp.bfloat16)
        prob = jax.nn.softmax(fresh, axis=-1)
        prob16 = prob.astype(jnp.bfloat16).astype(jnp.float32)
        attend = jnp.einsum("hqk,khd->qhd", prob16, v).reshape(TOKENS, INNER).astype(jnp.bfloat16)
        dattend = jnp.dot(g, w_out.T, preferred_element_type=jnp.float32).astype(jnp.bfloat16)
        dah = split_heads(dattend)
        dprob = jnp.einsum("qhd,khd->hqk", dah, v)
        delta = jnp.sum(dah * split_heads(attend), axis=-1).T
        dscore = (prob * (dprob - delta[:, :, None]) * scale).astype(jnp.bfloat16).astype(jnp.float32)
        dquery = jnp.einsum("hqk,khd->qhd", dscore, k).reshape(TOKENS, INNER).astype(jnp.bfloat16)
        blocks_q = q.reshape(N_PATCH, TOK_DEV, HEADS, HEAD_DIM)
        blocks_da = dah.reshape(N_PATCH, TOK_DEV, HEADS, HEAD_DIM)
        dkey = jnp.einsum("hpqk,pqhd->pkhd", dscore.reshape(HEADS, N_PATCH, TOK_DEV, TOKENS), blocks_q)
        dkey = dkey.astype(jnp.bfloat16).astype(jnp.float32).sum(0).reshape(TOKENS, INNER).astype(jnp.bfloat16)
        dvalue = jnp.einsum("hpqk,pqhd->pkhd", prob16.reshape(HEADS, N_PATCH, TOK_DEV, TOKENS), blocks_da)
        dvalue = dvalue.astype(jnp.bfloat16).astype(jnp.float32).sum(0).reshape(TOKENS, INNER).astype(jnp.bfloat16)
        grad_x = jnp.dot(dquery, w_query.T, preferred_element_type=jnp.float32)
        grad_x = grad_x + jnp.dot(dkey, w_key.T, preferred_element_type=jnp.float32)
        grad_x = grad_x + jnp.dot(dvalue, w_value.T, preferred_element_type=jnp.float32)
        grad_v = jnp.dot(x.T, dvalue, preferred_element_type=jnp.float32)
        grad_o = jnp.dot(attend.T, g, preferred_element_type=jnp.float32)
        return mixed, grad_x.astype(jnp.bfloat16), grad_v, grad_o

    mixed, grad_latents, grad_v, grad_o = lax.map(one_image, (latents_now, latents_stale, cotangent))
    return mixed, grad_latents, jnp.sum(grad_v, axis=0), jnp.sum(grad_o, axis=0)
```

```python
import jax
import jax.numpy as jnp
from jax import lax
from jax.experimental import pallas as pl
from jax.experimental.pallas import tpu as pltpu
from jax.sharding import PartitionSpec as P

HEADS = 10
HEAD_DIM = 64
N_PATCH = 8
N_IMG = 16
ROWS = 256
TOKENS = 2048
C = 1280
INNER = 640
PART = 832
SLOT = 208
HALF = 112
BF = jnp.bfloat16
F32 = jnp.float32
MESH = pl.DeviceIdType.MESH
NT = (((1,), (1,)), ((), ()))
NN = (((1,), (0,)), ((), ()))
SCALE = HEAD_DIM**-0.5
EXP2_SCALE = SCALE * 1.4426950408889634


def dot(a, b, dims=NN):
    return lax.dot_general(a, b, dims, preferred_element_type=F32)


def left_half(rows):
    return lax.broadcasted_iota(jnp.int32, (rows, 128), 1) < HEAD_DIM


def pair(a, b):
    return jnp.concatenate([a, b], axis=1)


def fresh_tile(qd, kv, acc_k, acc_v):
    left = left_half(ROWS)
    zero = jnp.zeros_like(qd)
    scores = dot(jnp.where(left, qd, zero), kv, NT)
    top = jnp.max(scores, axis=1, keepdims=True)
    e = jnp.exp2((scores - top) * EXP2_SCALE)
    inv = 1.0 / jnp.sum(e, axis=1, keepdims=True)
    e16 = e.astype(BF)
    a16 = (dot(e16, kv) * inv).astype(BF)
    delta = jnp.sum(
        jnp.where(left, 0.0, a16.astype(F32) * qd.astype(F32)), axis=1, keepdims=True
    )
    dprob = dot(jnp.where(left, zero, qd), kv, NT)
    ds = (e * (dprob - delta)).astype(BF)
    dq = dot(ds, kv) * (inv * SCALE)
    scaled = (qd.astype(F32) * jnp.where(left, inv * SCALE, inv)).T.astype(BF)
    acc_k[...] += dot(scaled[:HEAD_DIM], ds)
    acc_v[...] += dot(scaled[HEAD_DIM:], e16)
    return jnp.where(left, dq.astype(BF), a16)


def stale_tile(qd, kv):
    left = left_half(ROWS)
    scores = dot(jnp.where(left, qd, jnp.zeros_like(qd)), kv, NT)
    top = jnp.max(scores, axis=1, keepdims=True)
    e = jnp.exp2((scores - top) * EXP2_SCALE)
    inv = 1.0 / jnp.sum(e, axis=1, keepdims=True)
    out = (dot(e.astype(BF), kv) * inv).astype(BF)
    return pair(out[: ROWS // 2, HEAD_DIM:], out[ROWS // 2 :, HEAD_DIM:])


def kernel(
    x_hbm, s_hbm, wq_hbm, wk_hbm, wv_hbm, wo_hbm, g_hbm,
    mixed_ref, gradx_ref, gv_ref, go_ref,
    x, s, wq, wk, wv, wo, g, load_sem,
    st_kv, st_qd, st_ks, kv_w, qd_w, ks_w, kv_q, qd_q, ks_q,
    send_w, recv_w, send_q, recv_q, local_sem,
    acc_k, acc_v, kmix, out_w, out_q, dkv_w, dkv_q, att_w, att_q,
    home_a, home_d, home_p, home_t,
    rsend, rrecv, psend, precv,
    grads, from_core, from_y, ysum, from_xz, gathered, final,
    csem, ysend, yrecv, xsend, xrecv, gsend, grecv,
):
    img = lax.axis_index("img")
    me = lax.axis_index("patch")
    core = lax.rem(img, 2)
    zlo = lax.rem(img // 2, 2)
    yy = img // 4
    mine_e = me // 4
    first_q = 2 * lax.rem(me, 4)

    loads = []
    for n, (src, dst) in enumerate(
        ((x_hbm, x), (wk_hbm, wk), (wv_hbm, wv), (wq_hbm, wq), (g_hbm, g), (wo_hbm, wo), (s_hbm, s))
    ):
        copy = pltpu.make_async_copy(src, dst, load_sem.at[n])
        copy.start()
        loads.append(copy)

    barrier = pltpu.get_barrier_semaphore()
    for off in range(1, N_PATCH):
        pl.semaphore_signal(
            barrier, inc=1, device_id=(img, lax.rem(me + off, N_PATCH)), device_id_type=MESH
        )
    for off in range(1, N_IMG):
        pl.semaphore_signal(
            barrier, inc=1, device_id=(lax.rem(img + off, N_IMG), me), device_id_type=MESH
        )
    for off in range(1, N_PATCH):
        pl.semaphore_signal(
            barrier, inc=1,
            device_id=(img + 2 - 4 * zlo, lax.rem(me + off, N_PATCH)), device_id_type=MESH,
        )

    def to_whole(kind, stage, land, peer):
        return pltpu.make_async_remote_copy(
            src_ref=stage.at[peer], dst_ref=land.at[me],
            send_sem=send_w.at[kind, peer], recv_sem=recv_w.at[kind, me],
            device_id=(img, peer), device_id_type=MESH,
        )

    def from_whole(kind, land, peer):
        return pltpu.make_async_remote_copy(
            src_ref=land.at[peer], dst_ref=land.at[peer],
            send_sem=send_w.at[kind, peer], recv_sem=recv_w.at[kind, peer],
            device_id=(img, peer), device_id_type=MESH,
        )

    def to_quarter(kind, stage, land, peer):
        return pltpu.make_async_remote_copy(
            src_ref=stage.at[N_PATCH + peer // 4], dst_ref=land.at[me],
            send_sem=send_q.at[kind, peer], recv_sem=recv_q.at[kind, me],
            device_id=(img, peer), device_id_type=MESH,
        )

    def from_quarter(kind, land, peer):
        return pltpu.make_async_remote_copy(
            src_ref=land.at[peer], dst_ref=land.at[peer],
            send_sem=send_q.at[kind, peer], recv_sem=recv_q.at[kind, peer],
            device_id=(img, peer), device_id_type=MESH,
        )

    def quarter_rows(e):
        peer = 4 * e + me // 2
        return peer, pltpu.make_async_remote_copy(
            src_ref=st_qd.at[N_PATCH + e], dst_ref=qd_q.at[lax.rem(me, 2)],
            send_sem=send_q.at[1, e], recv_sem=recv_q.at[1, lax.rem(me, 2)],
            device_id=(img, peer), device_id_type=MESH,
        )

    def quarter_rows_in(t):
        return first_q + t, pltpu.make_async_remote_copy(
            src_ref=qd_q.at[t], dst_ref=qd_q.at[t],
            send_sem=send_q.at[1, t], recv_sem=recv_q.at[1, t],
            device_id=(img, first_q + t), device_id_type=MESH,
        )

    def peers(fn):
        def step(off, carry):
            fn(lax.rem(me + off, N_PATCH))
            return carry

        lax.fori_loop(1, N_PATCH, step, 0)

    def stage_pairs(stage, a, b):
        for h in range(HEADS):
            cols = slice(h * HEAD_DIM, (h + 1) * HEAD_DIM)
            stage[h] = pair(a[:, cols], b[:, cols])

    loads[0].wait()
    loads[1].wait()
    key = dot(x[...], wk[...]).astype(BF)
    loads[2].wait()
    value = dot(x[...], wv[...]).astype(BF)
    stage_pairs(st_kv, key, value)
    pl.semaphore_wait(barrier, 2 * (N_PATCH - 1) + N_IMG - 1)
    peers(lambda peer: to_whole(0, st_kv, kv_w, peer).start())
    kv_w[me] = st_kv[me]
    loads[3].wait()
    query = dot(x[...], wq[...]).astype(BF)
    loads[4].wait()
    loads[5].wait()
    dattend = dot(g[...], wo[...], NT).astype(BF)
    stage_pairs(st_qd, query, dattend)
    peers(lambda peer: to_whole(1, st_qd, qd_w, peer).start())
    qd_w[me] = st_qd[me]
    peers(lambda peer: to_quarter(0, st_kv, kv_q, peer).start())
    kv_q[me] = st_kv[N_PATCH + mine_e]
    for e in range(2):
        peer, copy = quarter_rows(e)

        @pl.when(peer != me)
        def _():
            copy.start()

        @pl.when(peer == me)
        def _():
            qd_q[lax.rem(me, 2)] = st_qd[N_PATCH + e]

    loads[6].wait()
    key_old = dot(s[...], wk[...]).astype(BF)
    value_old = dot(s[...], wv[...]).astype(BF)
    stage_pairs(st_ks, key_old, value_old)
    peers(lambda peer: to_whole(2, st_ks, ks_w, peer).start())
    ks_w[me] = st_ks[me]
    peers(lambda peer: to_quarter(2, st_ks, ks_q, peer).start())
    ks_q[me] = st_ks[N_PATCH + mine_e]

    def go_home(kind, src, land, peer):
        return pltpu.make_async_remote_copy(
            src_ref=src.at[peer], dst_ref=land.at[me],
            send_sem=rsend.at[kind, peer], recv_sem=rrecv.at[kind, me],
            device_id=(img, peer), device_id_type=MESH,
        )

    def come_home(kind, land, peer):
        return pltpu.make_async_remote_copy(
            src_ref=land.at[peer], dst_ref=land.at[peer],
            send_sem=rsend.at[kind, peer], recv_sem=rrecv.at[kind, peer],
            device_id=(img, peer), device_id_type=MESH,
        )

    def go_home_rows(kind, src, land, t):
        peer = first_q + t
        return peer, pltpu.make_async_remote_copy(
            src_ref=src.at[t], dst_ref=land.at[N_PATCH + mine_e],
            send_sem=psend.at[kind, t], recv_sem=precv.at[kind, mine_e],
            device_id=(img, peer), device_id_type=MESH,
        )

    def come_home_rows(kind, land, e):
        peer = 4 * e + me // 2
        return peer, pltpu.make_async_remote_copy(
            src_ref=land.at[N_PATCH + e], dst_ref=land.at[N_PATCH + e],
            send_sem=psend.at[kind, e], recv_sem=precv.at[kind, e],
            device_id=(img, peer), device_id_type=MESH,
        )

    def clear():
        acc_k[...] = jnp.zeros_like(acc_k)
        acc_v[...] = jnp.zeros_like(acc_v)

    def pack_dkv(out):
        for j in range(N_PATCH):
            cols = slice(j * ROWS, (j + 1) * ROWS)
            out[j] = pair(acc_k[:, cols].T.astype(BF), acc_v[:, cols].T.astype(BF))

    peers(lambda peer: from_whole(0, kv_w, peer).wait_recv())
    peers(lambda peer: from_whole(1, qd_w, peer).wait_recv())
    clear()

    def fresh_step(i, carry):
        out_w[i] = fresh_tile(qd_w[i], kv_w[...].reshape(TOKENS, 128), acc_k, acc_v)

        @pl.when(i != me)
        def _():
            go_home(0, out_w, home_a, i).start()

        return carry

    lax.fori_loop(0, N_PATCH, fresh_step, 0)
    home_a[me] = out_w[me]
    pack_dkv(dkv_w)
    peers(lambda peer: go_home(1, dkv_w, home_d, peer).start())
    home_d[me] = dkv_w[me]

    peers(lambda peer: from_quarter(0, kv_q, peer).wait_recv())
    for t in range(2):
        peer, copy = quarter_rows_in(t)

        @pl.when(peer != me)
        def _():
            copy.wait_recv()

    clear()

    def fresh_quarter_step(t, carry):
        out_q[t] = fresh_tile(qd_q[t], kv_q[...].reshape(TOKENS, 128), acc_k, acc_v)
        return carry

    lax.fori_loop(0, 2, fresh_quarter_step, 0)
    pack_dkv(dkv_q)

    def send_rows(kind, src, land):
        for t in range(2):
            peer, copy = go_home_rows(kind, src, land, t)

            @pl.when(peer != me)
            def _():
                copy.start()

            @pl.when(peer == me)
            def _():
                land[N_PATCH + mine_e] = src[t]

    send_rows(0, out_q, home_a)
    peers(lambda peer: go_home(2, dkv_q, home_p, peer).start())
    home_p[me] = dkv_q[me]

    peers(lambda peer: from_whole(2, ks_w, peer).wait_recv())
    kmix[...] = ks_w[...]

    def stale_step(i, carry):
        kmix[i] = kv_w[i]
        att_w[i] = stale_tile(qd_w[i], kmix[...].reshape(TOKENS, 128))
        kmix[i] = ks_w[i]

        @pl.when(i != me)
        def _():
            go_home(3, att_w, home_t, i).start()

        return carry

    lax.fori_loop(0, N_PATCH, stale_step, 0)
    home_t[me] = att_w[me]

    def receive_rows(kind, land):
        for e in range(2):
            peer, copy = come_home_rows(kind, land, e)

            @pl.when(peer != me)
            def _():
                copy.wait_recv()

    peers(lambda peer: come_home(0, home_a, peer).wait_recv())
    peers(lambda peer: come_home(1, home_d, peer).wait_recv())
    peers(lambda peer: come_home(2, home_p, peer).wait_recv())
    receive_rows(0, home_a)
    for e in range(2):
        total = home_p[4 * e].astype(F32)
        for n in range(1, 4):
            total = total + home_p[4 * e + n].astype(F32)
        home_d[N_PATCH + e] = total.astype(BF)

    def gather_heads(src, lo):
        return jnp.concatenate([src[h][:, lo : lo + HEAD_DIM] for h in range(HEADS)], axis=1)

    attend_t = gather_heads(home_a, HEAD_DIM).T
    dvalue = gather_heads(home_d, HEAD_DIM)
    x_t = x[...].T
    for q in range(N_PATCH):
        part = dot(x_t[160 * q : 160 * q + 160], dvalue).astype(BF)
        for c in range(5):
            grads[0, q, 160 * c : 160 * c + 160] = part[:, 128 * c : 128 * c + 128]
        part = dot(attend_t[80 * q : 80 * q + 80], g[...]).astype(BF)
        for c in range(10):
            grads[1, q, 80 * c : 80 * c + 80] = part[:, 128 * c : 128 * c + 128]
        grads[:, q, 800:] = jnp.zeros((2, PART - 800, 128), BF)

    core_copy = pltpu.make_async_remote_copy(
        src_ref=grads.at[1 - core], dst_ref=from_core,
        send_sem=csem.at[0], recv_sem=csem.at[1],
        device_id=(img + 1 - 2 * core, me), device_id_type=MESH,
    )
    core_copy.start()

    peers(lambda peer: from_quarter(2, ks_q, peer).wait_recv())
    kmix[...] = ks_q[...]

    def stale_quarter_step(t, carry):
        i = first_q + t
        kmix[i] = kv_q[i]
        att_q[t] = stale_tile(qd_q[t], kmix[...].reshape(TOKENS, 128))
        kmix[i] = ks_q[i]
        return carry

    lax.fori_loop(0, 2, stale_quarter_step, 0)
    send_rows(1, att_q, home_t)

    core_copy.wait()

    def core_add(q, carry):
        grads[core, q] = (grads[core, q].astype(F32) + from_core[q].astype(F32)).astype(BF)
        return carry

    lax.fori_loop(0, N_PATCH, core_add, 0)

    def y_copy(off):
        peer = lax.rem(yy + off, 4)
        return pltpu.make_async_remote_copy(
            src_ref=grads.at[core, :, pl.ds(pl.multiple_of(SLOT * peer, 16), SLOT)],
            dst_ref=from_y.at[off - 1],
            send_sem=ysend.at[off - 1], recv_sem=yrecv.at[off - 1],
            device_id=(4 * peer + 2 * zlo + core, me), device_id_type=MESH,
        )

    for off in range(1, 4):
        y_copy(off).start()

    dquery = gather_heads(home_a, 0)
    dkey = gather_heads(home_d, 0)
    gradx_ref[0] = (
        dot(dquery, wq[...], NT) + dot(dkey, wk[...], NT) + dot(dvalue, wv[...], NT)
    ).astype(BF)
    peers(lambda peer: come_home(3, home_t, peer).wait_recv())
    receive_rows(1, home_t)
    for r in range(2):
        rows = slice(r * ROWS // 2, (r + 1) * ROWS // 2)
        mixed_ref[0, rows] = dot(gather_heads(home_t, r * HEAD_DIM), wo[...]).astype(BF)

    for off in range(1, 4):
        y_copy(off).wait_recv()

    def y_add(q, carry):
        total = grads[core, q, pl.ds(pl.multiple_of(SLOT * yy, 16), SLOT)].astype(F32)
        for n in range(3):
            total = total + from_y[n, q].astype(F32)
        ysum[q, :SLOT] = total.astype(BF)
        ysum[q, SLOT:] = jnp.zeros((2 * HALF - SLOT, 128), BF)
        return carry

    lax.fori_loop(0, N_PATCH, y_add, 0)

    plane = zlo * N_PATCH + me

    def xz_peer(off):
        there = lax.rem(plane + off, 16)
        z_there, p_there = there // N_PATCH, lax.rem(there, N_PATCH)
        return there, z_there, p_there

    def xz_send(off):
        there, z_there, p_there = xz_peer(off)
        return pltpu.make_async_remote_copy(
            src_ref=ysum.at[p_there, pl.ds(pl.multiple_of(HALF * z_there, 16), HALF)],
            dst_ref=from_xz.at[plane],
            send_sem=xsend.at[there], recv_sem=xrecv.at[plane],
            device_id=(4 * yy + 2 * z_there + core, p_there), device_id_type=MESH,
        )

    def xz_recv(off):
        there, z_there, p_there = xz_peer(off)
        return pltpu.make_async_remote_copy(
            src_ref=from_xz.at[there], dst_ref=from_xz.at[there],
            send_sem=xsend.at[there], recv_sem=xrecv.at[there],
            device_id=(4 * yy + 2 * z_there + core, p_there), device_id_type=MESH,
        )

    def loop(lo, hi, fn):
        def step(n, carry):
            fn(n)
            return carry

        lax.fori_loop(lo, hi, step, 0)

    loop(1, 16, lambda off: xz_send(off).start())
    from_xz[plane] = ysum[me, pl.ds(pl.multiple_of(HALF * zlo, 16), HALF)]
    loop(1, 16, lambda off: xz_recv(off).wait_recv())
    total = from_xz[0].astype(F32)
    for n in range(1, 16):
        total = total + from_xz[n].astype(F32)
    gathered[img] = total.astype(BF)

    def gather_send(off):
        peer = lax.rem(img + off, N_IMG)
        return pltpu.make_async_remote_copy(
            src_ref=gathered.at[img], dst_ref=gathered.at[img],
            send_sem=gsend.at[peer], recv_sem=grecv.at[img],
            device_id=(peer, me), device_id_type=MESH,
        )

    def gather_recv(off):
        peer = lax.rem(img + off, N_IMG)
        return pltpu.make_async_remote_copy(
            src_ref=gathered.at[peer], dst_ref=gathered.at[peer],
            send_sem=gsend.at[peer], recv_sem=grecv.at[peer],
            device_id=(peer, me), device_id_type=MESH,
        )

    loop(1, N_IMG, lambda off: gather_send(off).start())
    loop(1, N_IMG, lambda off: gather_recv(off).wait_recv())
    for kind in range(2):
        for n in range(4):
            final[kind, SLOT * n : SLOT * n + HALF] = gathered[4 * n + kind].astype(F32)
            final[kind, SLOT * n + HALF : SLOT * (n + 1)] = gathered[4 * n + 2 + kind][
                : SLOT - HALF
            ].astype(F32)
    for c in range(5):
        gv_ref[:, 128 * c : 128 * c + 128] = final[0, 160 * c : 160 * c + 160]
    for c in range(10):
        go_ref[:, 128 * c : 128 * c + 128] = final[1, 80 * c : 80 * c + 80]

    for kind, (stage, land) in enumerate(((st_kv, kv_w), (st_qd, qd_w), (st_ks, ks_w))):
        peers(lambda peer: to_whole(kind, stage, land, peer).wait_send())
    for kind, stage, land in ((0, st_kv, kv_q), (2, st_ks, ks_q)):
        peers(lambda peer: to_quarter(kind, stage, land, peer).wait_send())
    for e in range(2):
        peer, copy = quarter_rows(e)

        @pl.when(peer != me)
        def _():
            copy.wait_send()

    for kind, src, land in ((0, out_w, home_a), (1, dkv_w, home_d), (2, dkv_q, home_p), (3, att_w, home_t)):
        peers(lambda peer: go_home(kind, src, land, peer).wait_send())
    for kind, src, land in ((0, out_q, home_a), (1, att_q, home_t)):
        for t in range(2):
            peer, copy = go_home_rows(kind, src, land, t)

            @pl.when(peer != me)
            def _():
                copy.wait_send()

    for off in range(1, 4):
        y_copy(off).wait_send()
    loop(1, 16, lambda off: xz_send(off).wait_send())
    loop(1, N_IMG, lambda off: gather_send(off).wait_send())


def vm(*shape, dtype=BF):
    return pltpu.VMEM(shape, dtype)


def dma(*shape):
    return pltpu.SemaphoreType.DMA(shape)


def on_device(latents_now, latents_stale, w_query, w_key, w_value, w_out, cotangent):
    return pl.pallas_call(
        kernel,
        out_shape=(
            jax.ShapeDtypeStruct((1, ROWS, C), BF),
            jax.ShapeDtypeStruct((1, ROWS, C), BF),
            jax.ShapeDtypeStruct((C // N_PATCH, INNER), F32),
            jax.ShapeDtypeStruct((INNER // N_PATCH, C), F32),
        ),
        in_specs=[pl.BlockSpec(memory_space=pl.ANY)] * 7,
        out_specs=[pl.BlockSpec(memory_space=pltpu.VMEM)] * 4,
        scratch_shapes=[
            vm(ROWS, C), vm(ROWS, C), vm(C, INNER), vm(C, INNER), vm(C, INNER), vm(INNER, C), vm(ROWS, C),
            dma(7),
            vm(10, ROWS, 128), vm(10, ROWS, 128), vm(10, ROWS, 128),
            vm(8, ROWS, 128), vm(8, ROWS, 128), vm(8, ROWS, 128),
            vm(8, ROWS, 128), vm(2, ROWS, 128), vm(8, ROWS, 128),
            dma(3, 8), dma(3, 8), dma(3, 8), dma(3, 8), dma(1),
            vm(HEAD_DIM, TOKENS, dtype=F32), vm(HEAD_DIM, TOKENS, dtype=F32),
            vm(8, ROWS, 128), vm(8, ROWS, 128), vm(2, ROWS, 128),
            vm(8, ROWS, 128), vm(8, ROWS, 128), vm(8, ROWS // 2, 128), vm(2, ROWS // 2, 128),
            vm(10, ROWS, 128), vm(10, ROWS, 128), vm(8, ROWS, 128), vm(10, ROWS // 2, 128),
            dma(4, 8), dma(4, 8), dma(2, 2), dma(2, 2),
            vm(2, 8, PART, 128), vm(8, PART, 128), vm(3, 8, SLOT, 128), vm(8, 2 * HALF, 128),
            vm(16, HALF, 128), vm(16, HALF, 128), vm(2, PART, 128, dtype=F32),
            dma(2), dma(3), dma(3), dma(16), dma(16), dma(16), dma(16),
        ],
        compiler_params=pltpu.CompilerParams(
            collective_id=0, has_side_effects=True, vmem_limit_bytes=56 * 2**20
        ),
        cost_estimate=pl.CostEstimate(flops=10**10, bytes_accessed=12 * 2**20, transcendentals=10**7),
    )(latents_now[0], latents_stale[0], w_query, w_key, w_value, w_out, cotangent[0])


def solution(mesh):
    rows = P("img", "patch", None)
    return jax.shard_map(
        on_device,
        mesh=mesh,
        in_specs=(rows, rows, P(), P(), P(), P(), rows),
        out_specs=(rows, rows, P("patch", None), P("patch", None)),
        check_vma=False,
    )
```

```python
import jax
import jax.numpy as jnp
from jax import lax
from jax.experimental import pallas as pl
from jax.experimental.pallas import tpu as pltpu
from jax.sharding import PartitionSpec as P

HEADS = 10
HEAD_DIM = 64
N_PATCH = 8
N_IMG = 16
ROWS = 256
TOKENS = 2048
C = 1280
INNER = 640
PART = 832
SLOT = 208
HALF = 112
BF = jnp.bfloat16
F32 = jnp.float32
MESH = pl.DeviceIdType.MESH
NT = (((1,), (1,)), ((), ()))
NN = (((1,), (0,)), ((), ()))
SCALE = HEAD_DIM**-0.5
EXP2_SCALE = SCALE * 1.4426950408889634


def dot(a, b, dims=NN):
    return lax.dot_general(a, b, dims, preferred_element_type=F32)


def left_half(rows):
    return lax.broadcasted_iota(jnp.int32, (rows, 128), 1) < HEAD_DIM


def pair(a, b):
    return jnp.concatenate([a, b], axis=1)


def fold(x, lo):
    cols = slice(lo, lo + HEAD_DIM)
    return pair(x[: ROWS // 2, cols], x[ROWS // 2 :, cols])


def probabilities(qd, kv):
    left = left_half(ROWS)
    scores = dot(jnp.where(left, qd, jnp.zeros_like(qd)), kv, NT)
    top = jnp.max(scores, axis=1, keepdims=True)
    e = jnp.exp2((scores - top) * EXP2_SCALE)
    inv = 1.0 / jnp.sum(e, axis=1, keepdims=True)
    return e.astype(BF), inv


def fresh_first(qd, kv, acc):
    left = left_half(ROWS)
    e16, inv = probabilities(qd, kv)
    a16 = (dot(e16, kv) * inv).astype(BF)
    delta = jnp.sum(
        jnp.where(left, 0.0, a16.astype(F32) * qd.astype(F32)), axis=1, keepdims=True
    )
    scaled = (qd.astype(F32) * jnp.where(left, inv * SCALE, inv)).T.astype(BF)
    acc[...] += dot(scaled[HEAD_DIM:], e16)
    return e16, fold(a16, HEAD_DIM), jnp.where(left, inv * SCALE, delta), scaled[:HEAD_DIM]


def fresh_second(qd, kv, e16, stats, q_scaled, acc):
    left = left_half(ROWS)
    dprob = dot(jnp.where(left, jnp.zeros_like(qd), qd), kv, NT)
    ds = (e16.astype(F32) * (dprob - stats[:, HEAD_DIM : HEAD_DIM + 1])).astype(BF)
    dq = dot(ds, kv) * stats[:, 0:1]
    acc[...] += dot(q_scaled, ds)
    return fold(dq.astype(BF), 0)


def stale_tile(qd, kv):
    e16, inv = probabilities(qd, kv)
    return fold((dot(e16, kv) * inv).astype(BF), HEAD_DIM)


def loop(lo, hi, fn):
    def step(n, carry):
        fn(n)
        return carry

    lax.fori_loop(lo, hi, step, 0)


def kernel(
    x_hbm, s_hbm, wq_hbm, wk_hbm, wv_hbm, wo_hbm, g_hbm,
    mixed_out, gradx_out, gv_out, go_out,
    x2, g2, s, wq, wk, wv, wo, load_sem, share_sem,
    st_kv, st_qd, st_ks,
    kv_w, qd_w, ks_w, kv_q, qd_q, ks_q,
    send_w, recv_w, send_q, recv_q,
    e_w, e_q, stats, q_scaled, acc, kmix,
    out_a, out_dq, out_t, out_dv, out_dk, part_dv, part_dk, row_a, row_dq, row_t,
    home_a, home_dq, home_t, home_dv, home_dk, home_dvp, home_dkp,
    hsend, hrecv, psend, precv, asend, arecv, apsend, aprecv,
    x_t, dv2, grads, from_y, ysum, from_xz, gathered, final,
    mixed, gradx, gv, go,
    dsem, ysend, yrecv, xsend, xrecv, gsend, grecv, out_sem,
):
    img = lax.axis_index("img")
    me = lax.axis_index("patch")
    core = lax.rem(img, 2)
    zlo = lax.rem(img // 2, 2)
    yy = img // 4
    mine_e = me // 4
    first_q = 2 * lax.rem(me, 4)
    core_one = img - core + 1
    sibling = img + 1 - 2 * core

    loads = []
    for n, (src, dst) in enumerate(
        ((x_hbm, x2.at[core]), (wk_hbm, wk), (wv_hbm, wv), (wq_hbm, wq), (g_hbm, g2.at[core]), (wo_hbm, wo), (s_hbm, s))
    ):
        copy = pltpu.make_async_copy(src, dst, load_sem.at[n])
        copy.start()
        loads.append(copy)

    barrier = pltpu.get_barrier_semaphore()
    for off in range(1, N_PATCH):
        pl.semaphore_signal(
            barrier, inc=1, device_id=(img, lax.rem(me + off, N_PATCH)), device_id_type=MESH
        )
    for off in range(1, N_IMG):
        pl.semaphore_signal(
            barrier, inc=1, device_id=(lax.rem(img + off, N_IMG), me), device_id_type=MESH
        )
    for off in range(1, N_PATCH):
        for there in (img + 2 - 4 * zlo, sibling):
            pl.semaphore_signal(
                barrier, inc=1, device_id=(there, lax.rem(me + off, N_PATCH)), device_id_type=MESH
            )

    def peers(fn):
        for dz, dx in ((1, 1), (0, 1), (1, 3), (0, 3), (1, 0), (1, 2), (0, 2)):
            fn(lax.rem(me // 4 + dz, 2) * 4 + lax.rem(me + dx, 4))

    def to_whole(kind, stage, land, peer):
        return pltpu.make_async_remote_copy(
            src_ref=stage.at[peer], dst_ref=land.at[me],
            send_sem=send_w.at[kind, peer], recv_sem=recv_w.at[kind, me],
            device_id=(img, peer), device_id_type=MESH,
        )

    def from_whole(kind, land, peer):
        return pltpu.make_async_remote_copy(
            src_ref=land.at[peer], dst_ref=land.at[peer],
            send_sem=send_w.at[kind, peer], recv_sem=recv_w.at[kind, peer],
            device_id=(img, peer), device_id_type=MESH,
        )

    def to_quarter(kind, stage, land, peer):
        return pltpu.make_async_remote_copy(
            src_ref=stage.at[N_PATCH + peer // 4], dst_ref=land.at[me],
            send_sem=send_q.at[kind, peer], recv_sem=recv_q.at[kind, me],
            device_id=(img, peer), device_id_type=MESH,
        )

    def from_quarter(kind, land, peer):
        return pltpu.make_async_remote_copy(
            src_ref=land.at[peer], dst_ref=land.at[peer],
            send_sem=send_q.at[kind, peer], recv_sem=recv_q.at[kind, peer],
            device_id=(img, peer), device_id_type=MESH,
        )

    def quarter_rows(e):
        peer = 4 * e + me // 2
        return peer, pltpu.make_async_remote_copy(
            src_ref=st_qd.at[N_PATCH + e], dst_ref=qd_q.at[lax.rem(me, 2)],
            send_sem=send_q.at[1, e], recv_sem=recv_q.at[1, lax.rem(me, 2)],
            device_id=(img, peer), device_id_type=MESH,
        )

    def quarter_rows_in(t):
        return first_q + t, pltpu.make_async_remote_copy(
            src_ref=qd_q.at[t], dst_ref=qd_q.at[t],
            send_sem=send_q.at[1, t], recv_sem=recv_q.at[1, t],
            device_id=(img, first_q + t), device_id_type=MESH,
        )

    def share(core_from, ref, n):
        return pltpu.make_async_remote_copy(
            src_ref=ref.at[core_from], dst_ref=ref.at[core_from],
            send_sem=share_sem.at[n], recv_sem=share_sem.at[2 + n],
            device_id=(sibling, me), device_id_type=MESH,
        )

    def stage_pairs(stage, a, b):
        for h in range(HEADS):
            cols = slice(h * HEAD_DIM, (h + 1) * HEAD_DIM)
            stage[h] = pair(a[:, cols], b[:, cols])

    loads[0].wait()
    loads[1].wait()
    key = dot(x2[core], wk[...]).astype(BF)
    loads[2].wait()
    value = dot(x2[core], wv[...]).astype(BF)
    stage_pairs(st_kv, key, value)
    pl.semaphore_wait(barrier, 3 * (N_PATCH - 1) + N_IMG - 1)
    peers(lambda peer: to_whole(0, st_kv, kv_w, peer).start())
    kv_w[me] = st_kv[me]
    loads[3].wait()
    query = dot(x2[core], wq[...]).astype(BF)
    loads[4].wait()
    loads[5].wait()
    dattend = dot(g2[core], wo[...], NT).astype(BF)
    stage_pairs(st_qd, query, dattend)
    peers(lambda peer: to_whole(1, st_qd, qd_w, peer).start())
    qd_w[me] = st_qd[me]
    peers(lambda peer: to_quarter(0, st_kv, kv_q, peer).start())
    kv_q[me] = st_kv[N_PATCH + mine_e]
    for e in range(2):
        peer, copy = quarter_rows(e)

        @pl.when(peer != me)
        def _():
            copy.start()

        @pl.when(peer == me)
        def _():
            qd_q[lax.rem(me, 2)] = st_qd[N_PATCH + e]

    @pl.when(core == 1)
    def _():
        share(1, x2, 0).start()

    @pl.when(core == 0)
    def _():
        share(0, g2, 1).start()

    loads[6].wait()
    key_old = dot(s[...], wk[...]).astype(BF)
    value_old = dot(s[...], wv[...]).astype(BF)
    stage_pairs(st_ks, key_old, value_old)
    ks_w[me] = st_ks[me]
    ks_q[me] = st_ks[N_PATCH + mine_e]

    @pl.when(core == 0)
    def _():
        share(1, x2, 0).wait_recv()
        x_t[:, :ROWS] = x2[0].T
        x_t[:, ROWS:] = x2[1].T

    @pl.when(core == 1)
    def _():
        share(0, g2, 1).wait_recv()

    def go_home(kind, src, land, peer):
        return pltpu.make_async_remote_copy(
            src_ref=src.at[peer], dst_ref=land.at[me],
            send_sem=hsend.at[kind, peer], recv_sem=hrecv.at[kind, me],
            device_id=(img, peer), device_id_type=MESH,
        )

    def come_home(kind, land, peer):
        return pltpu.make_async_remote_copy(
            src_ref=land.at[peer], dst_ref=land.at[peer],
            send_sem=hsend.at[kind, peer], recv_sem=hrecv.at[kind, peer],
            device_id=(img, peer), device_id_type=MESH,
        )

    def go_home_rows(kind, src, land, t):
        peer = first_q + t
        return peer, pltpu.make_async_remote_copy(
            src_ref=src.at[t], dst_ref=land.at[N_PATCH + mine_e],
            send_sem=psend.at[kind, t], recv_sem=precv.at[kind, mine_e],
            device_id=(img, peer), device_id_type=MESH,
        )

    def come_home_rows(kind, land, e):
        peer = 4 * e + me // 2
        return peer, pltpu.make_async_remote_copy(
            src_ref=land.at[N_PATCH + e], dst_ref=land.at[N_PATCH + e],
            send_sem=psend.at[kind, e], recv_sem=precv.at[kind, e],
            device_id=(img, peer), device_id_type=MESH,
        )

    def a_home(i):
        return pltpu.make_async_remote_copy(
            src_ref=out_a.at[i], dst_ref=home_a.at[core, me],
            send_sem=asend.at[i], recv_sem=arecv.at[core, me],
            device_id=(core_one, i), device_id_type=MESH,
        )

    def a_in(c, peer):
        return pltpu.make_async_remote_copy(
            src_ref=home_a.at[c, peer], dst_ref=home_a.at[c, peer],
            send_sem=asend.at[peer], recv_sem=arecv.at[c, peer],
            device_id=(core_one, peer), device_id_type=MESH,
        )

    def a_home_rows(t):
        return pltpu.make_async_remote_copy(
            src_ref=row_a.at[t], dst_ref=home_a.at[core, N_PATCH + mine_e],
            send_sem=apsend.at[t], recv_sem=aprecv.at[core, mine_e],
            device_id=(core_one, first_q + t), device_id_type=MESH,
        )

    def a_in_rows(c, e):
        return pltpu.make_async_remote_copy(
            src_ref=home_a.at[c, N_PATCH + e], dst_ref=home_a.at[c, N_PATCH + e],
            send_sem=apsend.at[e], recv_sem=aprecv.at[c, e],
            device_id=(core_one, 4 * e + me // 2), device_id_type=MESH,
        )

    def stays(peer):
        return jnp.logical_and(peer == me, core == 1)

    def put(out):
        for j in range(N_PATCH):
            out[j] = fold(acc[:, j * ROWS : (j + 1) * ROWS].T.astype(BF), 0)

    def clear():
        acc[...] = jnp.zeros_like(acc)

    peers(lambda peer: from_whole(0, kv_w, peer).wait_recv())
    peers(lambda peer: from_whole(1, qd_w, peer).wait_recv())
    clear()

    def first_whole(i):
        e_w[i], out_a[i], stats[i], q_scaled[i] = fresh_first(
            qd_w[i], kv_w[...].reshape(TOKENS, 128), acc
        )

        @pl.when(jnp.logical_not(stays(i)))
        def _():
            a_home(i).start()

    loop(0, N_PATCH, first_whole)

    @pl.when(core == 1)
    def _():
        home_a[1, me] = out_a[me]

    put(out_dv)
    peers(lambda peer: go_home(3, out_dv, home_dv, peer).start())
    home_dv[me] = out_dv[me]
    peers(lambda peer: to_whole(2, st_ks, ks_w, peer).start())

    peers(lambda peer: from_quarter(0, kv_q, peer).wait_recv())
    for t in range(2):
        peer, copy = quarter_rows_in(t)

        @pl.when(peer != me)
        def _():
            copy.wait_recv()

    clear()

    def first_quarter(t):
        e_q[t], row_a[t], stats[N_PATCH + t], q_scaled[N_PATCH + t] = fresh_first(
            qd_q[t], kv_q[...].reshape(TOKENS, 128), acc
        )

    loop(0, 2, first_quarter)
    for t in range(2):
        here = stays(first_q + t)

        @pl.when(jnp.logical_not(here))
        def _():
            a_home_rows(t).start()

        @pl.when(here)
        def _():
            home_a[1, N_PATCH + mine_e] = row_a[t]

    put(part_dv)
    peers(lambda peer: go_home(5, part_dv, home_dvp, peer).start())
    home_dvp[me] = part_dv[me]
    peers(lambda peer: to_quarter(2, st_ks, ks_q, peer).start())

    clear()

    def second_whole(i):
        out_dq[i] = fresh_second(
            qd_w[i], kv_w[...].reshape(TOKENS, 128), e_w[i], stats[i], q_scaled[i], acc
        )

        @pl.when(i != me)
        def _():
            go_home(0, out_dq, home_dq, i).start()

    loop(0, N_PATCH, second_whole)
    home_dq[me] = out_dq[me]
    put(out_dk)
    peers(lambda peer: go_home(1, out_dk, home_dk, peer).start())
    home_dk[me] = out_dk[me]

    def unfold(src, r):
        cols = slice(r * HEAD_DIM, (r + 1) * HEAD_DIM)
        return jnp.concatenate([src[h][:, cols] for h in range(HEADS)], axis=1)

    def add_shared(land, parts):
        for e in range(2):
            total = parts[4 * e].astype(F32)
            for n in range(1, 4):
                total = total + parts[4 * e + n].astype(F32)
            land[N_PATCH + e] = total.astype(BF)

    peers(lambda peer: come_home(3, home_dv, peer).wait_recv())
    peers(lambda peer: come_home(5, home_dvp, peer).wait_recv())
    add_shared(home_dv, home_dvp)
    for r in range(2):
        dv2[core, r * ROWS // 2 : (r + 1) * ROWS // 2] = unfold(home_dv, r)
    dv_share = pltpu.make_async_remote_copy(
        src_ref=dv2.at[1], dst_ref=dv2.at[1], send_sem=dsem.at[0], recv_sem=dsem.at[1],
        device_id=(sibling, me), device_id_type=MESH,
    )

    @pl.when(core == 1)
    def _():
        dv_share.start()
        for c in range(2):
            for n in range(N_PATCH):
                if c == 1:
                    @pl.when(n != me)
                    def _():
                        a_in(c, n).wait_recv()
                else:
                    a_in(c, n).wait_recv()
            for e in range(2):
                if c == 1:
                    @pl.when(4 * e + me // 2 != me)
                    def _():
                        a_in_rows(c, e).wait_recv()
                else:
                    a_in_rows(c, e).wait_recv()
        a_t = jnp.concatenate(
            [unfold(home_a.at[c], r).T for c in range(2) for r in range(2)], axis=1
        )
        g_all = g2[...].reshape(2 * ROWS, C)
        for q in range(N_PATCH):
            part = dot(a_t[80 * q : 80 * q + 80], g_all).astype(BF)
            for c in range(10):
                grads[q, 80 * c : 80 * c + 80] = part[:, 128 * c : 128 * c + 128]

    @pl.when(core == 0)
    def _():
        dv_share.wait_recv()
        dv_all = dv2[...].reshape(2 * ROWS, INNER)
        for q in range(N_PATCH):
            part = dot(x_t[160 * q : 160 * q + 160], dv_all).astype(BF)
            for c in range(5):
                grads[q, 160 * c : 160 * c + 160] = part[:, 128 * c : 128 * c + 128]

    grads[:, 800:] = jnp.zeros((N_PATCH, PART - 800, 128), BF)

    def y_copy(off):
        peer = lax.rem(yy + off, 4)
        return pltpu.make_async_remote_copy(
            src_ref=grads.at[:, pl.ds(pl.multiple_of(SLOT * peer, 16), SLOT)],
            dst_ref=from_y.at[off - 1],
            send_sem=ysend.at[off - 1], recv_sem=yrecv.at[off - 1],
            device_id=(4 * peer + 2 * zlo + core, me), device_id_type=MESH,
        )

    for off in range(1, 4):
        y_copy(off).start()

    clear()

    def second_quarter(t):
        row_dq[t] = fresh_second(
            qd_q[t], kv_q[...].reshape(TOKENS, 128), e_q[t], stats[N_PATCH + t],
            q_scaled[N_PATCH + t], acc,
        )

    loop(0, 2, second_quarter)

    def send_rows(kind, src, land):
        for t in range(2):
            peer, copy = go_home_rows(kind, src, land, t)

            @pl.when(peer != me)
            def _():
                copy.start()

            @pl.when(peer == me)
            def _():
                land[N_PATCH + mine_e] = src[t]

    send_rows(0, row_dq, home_dq)
    put(part_dk)
    peers(lambda peer: go_home(4, part_dk, home_dkp, peer).start())
    home_dkp[me] = part_dk[me]

    peers(lambda peer: from_whole(2, ks_w, peer).wait_recv())
    kmix[...] = ks_w[...]

    def stale_whole(i):
        kmix[i] = kv_w[i]
        out_t[i] = stale_tile(qd_w[i], kmix[...].reshape(TOKENS, 128))
        kmix[i] = ks_w[i]

        @pl.when(i != me)
        def _():
            go_home(2, out_t, home_t, i).start()

    loop(0, N_PATCH, stale_whole)
    home_t[me] = out_t[me]
    peers(lambda peer: from_quarter(2, ks_q, peer).wait_recv())
    kmix[...] = ks_q[...]

    def stale_quarter(t):
        i = first_q + t
        kmix[i] = kv_q[i]
        row_t[t] = stale_tile(qd_q[t], kmix[...].reshape(TOKENS, 128))
        kmix[i] = ks_q[i]

    loop(0, 2, stale_quarter)
    send_rows(1, row_t, home_t)

    for off in range(1, 4):
        y_copy(off).wait_recv()

    def y_add(q):
        total = grads[q, pl.ds(pl.multiple_of(SLOT * yy, 16), SLOT)].astype(F32)
        for n in range(3):
            total = total + from_y[n, q].astype(F32)
        ysum[q, :SLOT] = total.astype(BF)
        ysum[q, SLOT:] = jnp.zeros((2 * HALF - SLOT, 128), BF)

    loop(0, N_PATCH, y_add)
    plane = zlo * N_PATCH + me

    def xz_peer(off):
        there = lax.rem(plane + off, 16)
        return there, there // N_PATCH, lax.rem(there, N_PATCH)

    def xz_send(off):
        there, z_there, p_there = xz_peer(off)
        return pltpu.make_async_remote_copy(
            src_ref=ysum.at[p_there, pl.ds(pl.multiple_of(HALF * z_there, 16), HALF)],
            dst_ref=from_xz.at[plane],
            send_sem=xsend.at[there], recv_sem=xrecv.at[plane],
            device_id=(4 * yy + 2 * z_there + core, p_there), device_id_type=MESH,
        )

    def xz_recv(off):
        there, z_there, p_there = xz_peer(off)
        return pltpu.make_async_remote_copy(
            src_ref=from_xz.at[there], dst_ref=from_xz.at[there],
            send_sem=xsend.at[there], recv_sem=xrecv.at[there],
            device_id=(4 * yy + 2 * z_there + core, p_there), device_id_type=MESH,
        )

    loop(1, 16, lambda off: xz_send(off).start())
    from_xz[plane] = ysum[me, pl.ds(pl.multiple_of(HALF * zlo, 16), HALF)]

    def receive_rows(kind, land):
        for e in range(2):
            peer, copy = come_home_rows(kind, land, e)

            @pl.when(peer != me)
            def _():
                copy.wait_recv()

    peers(lambda peer: come_home(0, home_dq, peer).wait_recv())
    receive_rows(0, home_dq)
    peers(lambda peer: come_home(1, home_dk, peer).wait_recv())
    peers(lambda peer: come_home(4, home_dkp, peer).wait_recv())
    add_shared(home_dk, home_dkp)
    dquery = jnp.concatenate([unfold(home_dq, 0), unfold(home_dq, 1)], axis=0)
    dkey = jnp.concatenate([unfold(home_dk, 0), unfold(home_dk, 1)], axis=0)
    gradx[...] = (
        dot(dquery, wq[...], NT) + dot(dkey, wk[...], NT) + dot(dv2[core], wv[...], NT)
    ).astype(BF)
    gradx_copy = pltpu.make_async_copy(gradx, gradx_out.at[0], out_sem.at[0])
    gradx_copy.start()

    loop(1, 16, lambda off: xz_recv(off).wait_recv())
    total = from_xz[0].astype(F32)
    for n in range(1, 16):
        total = total + from_xz[n].astype(F32)
    gathered[img] = total.astype(BF)

    def gather_send(off):
        peer = lax.rem(img + off, N_IMG)
        return pltpu.make_async_remote_copy(
            src_ref=gathered.at[img], dst_ref=gathered.at[img],
            send_sem=gsend.at[peer], recv_sem=grecv.at[img],
            device_id=(peer, me), device_id_type=MESH,
        )

    def gather_recv(off):
        peer = lax.rem(img + off, N_IMG)
        return pltpu.make_async_remote_copy(
            src_ref=gathered.at[peer], dst_ref=gathered.at[peer],
            send_sem=gsend.at[peer], recv_sem=grecv.at[peer],
            device_id=(peer, me), device_id_type=MESH,
        )

    loop(1, N_IMG, lambda off: gather_send(off).start())

    peers(lambda peer: come_home(2, home_t, peer).wait_recv())
    receive_rows(1, home_t)
    for r in range(2):
        mixed[r * ROWS // 2 : (r + 1) * ROWS // 2] = dot(unfold(home_t, r), wo[...]).astype(BF)
    mixed_copy = pltpu.make_async_copy(mixed, mixed_out.at[0], out_sem.at[1])
    mixed_copy.start()

    loop(1, N_IMG, lambda off: gather_recv(off).wait_recv())
    for kind in range(2):
        for n in range(4):
            final[kind, SLOT * n : SLOT * n + HALF] = gathered[4 * n + kind].astype(F32)
            final[kind, SLOT * n + HALF : SLOT * (n + 1)] = gathered[4 * n + 2 + kind][
                : SLOT - HALF
            ].astype(F32)
    for c in range(5):
        gv[:, 128 * c : 128 * c + 128] = final[0, 160 * c : 160 * c + 160]
    for c in range(10):
        go[:, 128 * c : 128 * c + 128] = final[1, 80 * c : 80 * c + 80]
    gv_copy = pltpu.make_async_copy(gv, gv_out, out_sem.at[2])
    go_copy = pltpu.make_async_copy(go, go_out, out_sem.at[3])
    gv_copy.start()
    go_copy.start()

    for kind, stage, land in ((0, st_kv, kv_w), (1, st_qd, qd_w), (2, st_ks, ks_w)):
        peers(lambda peer: to_whole(kind, stage, land, peer).wait_send())
    for kind, stage, land in ((0, st_kv, kv_q), (2, st_ks, ks_q)):
        peers(lambda peer: to_quarter(kind, stage, land, peer).wait_send())
    for e in range(2):
        peer, copy = quarter_rows(e)

        @pl.when(peer != me)
        def _():
            copy.wait_send()

    @pl.when(core == 1)
    def _():
        share(1, x2, 0).wait_send()
        dv_share.wait_send()

    @pl.when(core == 0)
    def _():
        share(0, g2, 1).wait_send()

    for kind, src, land in (
        (0, out_dq, home_dq), (1, out_dk, home_dk), (2, out_t, home_t),
        (3, out_dv, home_dv), (4, part_dk, home_dkp), (5, part_dv, home_dvp),
    ):
        peers(lambda peer: go_home(kind, src, land, peer).wait_send())
    for kind, src, land in ((0, row_dq, home_dq), (1, row_t, home_t)):
        for t in range(2):
            peer, copy = go_home_rows(kind, src, land, t)

            @pl.when(peer != me)
            def _():
                copy.wait_send()

    for n in range(N_PATCH):
        @pl.when(jnp.logical_not(stays(n)))
        def _():
            a_home(n).wait_send()

    for t in range(2):
        @pl.when(jnp.logical_not(stays(first_q + t)))
        def _():
            a_home_rows(t).wait_send()

    for off in range(1, 4):
        y_copy(off).wait_send()
    loop(1, 16, lambda off: xz_send(off).wait_send())
    loop(1, N_IMG, lambda off: gather_send(off).wait_send())
    for copy in (gradx_copy, mixed_copy, gv_copy, go_copy):
        copy.wait()


def pass_on(*refs):
    sources, results, held = refs[:4], refs[4:8], refs[8:12]
    load_sem, store_sem = refs[12:]
    loads = [pltpu.make_async_copy(sources[n], held[n], load_sem.at[n]) for n in range(4)]
    stores = [pltpu.make_async_copy(held[n], results[n], store_sem.at[n]) for n in range(4)]
    for copy in loads:
        copy.start()
    for load, store in zip(loads, stores):
        load.wait()
        store.start()
    for store in stores:
        store.wait()


def vm(*shape, dtype=BF):
    return pltpu.VMEM(shape, dtype)


def dma(*shape):
    return pltpu.SemaphoreType.DMA(shape)


def on_device(latents_now, latents_stale, w_query, w_key, w_value, w_out, cotangent):
    half = ROWS // 2
    shapes = (
        jax.ShapeDtypeStruct((1, ROWS, C), BF),
        jax.ShapeDtypeStruct((1, ROWS, C), BF),
        jax.ShapeDtypeStruct((C // N_PATCH, INNER), F32),
        jax.ShapeDtypeStruct((INNER // N_PATCH, C), F32),
    )
    anywhere = pl.BlockSpec(memory_space=pl.ANY)
    results = pl.pallas_call(
        kernel,
        out_shape=shapes,
        in_specs=[anywhere] * 7,
        out_specs=[anywhere] * 4,
        scratch_shapes=[
            vm(2, ROWS, C), vm(2, ROWS, C), vm(ROWS, C), vm(C, INNER), vm(C, INNER), vm(C, INNER), vm(INNER, C),
            dma(7), dma(4),
            vm(10, ROWS, 128), vm(10, ROWS, 128), vm(10, ROWS, 128),
            vm(8, ROWS, 128), vm(8, ROWS, 128), vm(8, ROWS, 128),
            vm(8, ROWS, 128), vm(2, ROWS, 128), vm(8, ROWS, 128),
            dma(3, 8), dma(3, 8), dma(3, 8), dma(3, 8),
            vm(8, ROWS, TOKENS), vm(2, ROWS, TOKENS), vm(10, ROWS, 128, dtype=F32), vm(10, HEAD_DIM, ROWS),
            vm(HEAD_DIM, TOKENS, dtype=F32), vm(8, ROWS, 128),
            vm(8, half, 128), vm(8, half, 128), vm(8, half, 128), vm(8, half, 128), vm(8, half, 128),
            vm(8, half, 128), vm(8, half, 128), vm(2, half, 128), vm(2, half, 128), vm(2, half, 128),
            vm(2, 10, half, 128), vm(10, half, 128), vm(10, half, 128), vm(10, half, 128), vm(10, half, 128),
            vm(8, half, 128), vm(8, half, 128),
            dma(6, 8), dma(6, 8), dma(2, 2), dma(2, 2), dma(8), dma(2, 8), dma(2), dma(2, 2),
            vm(C, 2 * ROWS), vm(2, ROWS, INNER), vm(8, PART, 128), vm(3, 8, SLOT, 128), vm(8, 2 * HALF, 128),
            vm(16, HALF, 128), vm(16, HALF, 128), vm(2, PART, 128, dtype=F32),
            vm(ROWS, C), vm(ROWS, C), vm(C // N_PATCH, INNER, dtype=F32), vm(INNER // N_PATCH, C, dtype=F32),
            dma(2), dma(3), dma(3), dma(16), dma(16), dma(16), dma(16), dma(4),
        ],
        compiler_params=pltpu.CompilerParams(
            collective_id=0, has_side_effects=True, vmem_limit_bytes=56 * 2**20
        ),
        cost_estimate=pl.CostEstimate(flops=10**10, bytes_accessed=12 * 2**20, transcendentals=10**7),
    )(latents_now[0], latents_stale[0], w_query, w_key, w_value, w_out, cotangent[0])
    return pl.pallas_call(
        pass_on,
        out_shape=shapes,
        in_specs=[anywhere] * 4,
        out_specs=[anywhere] * 4,
        scratch_shapes=[pltpu.VMEM(shape.shape, shape.dtype) for shape in shapes] + [dma(4), dma(4)],
        compiler_params=pltpu.CompilerParams(vmem_limit_bytes=16 * 2**20),
        cost_estimate=pl.CostEstimate(flops=0, bytes_accessed=2 * 2**20, transcendentals=0),
    )(*results)


def solution(mesh):
    rows = P("img", "patch", None)
    return jax.shard_map(
        on_device,
        mesh=mesh,
        in_specs=(rows, rows, P(), P(), P(), P(), rows),
        out_specs=(rows, rows, P("patch", None), P("patch", None)),
        check_vma=False,
    )
```

```python
import jax
import jax.numpy as jnp
from jax import lax
from jax.experimental import pallas as pl
from jax.experimental.pallas import tpu as pltpu
from jax.sharding import PartitionSpec as P

HEADS = 10
HEAD_DIM = 64
N_PATCH = 8
N_IMG = 16
ROWS = 256
TOKENS = 2048
C = 1280
INNER = 640
PART = 832
SLOT = 208
HALF = 112
BF = jnp.bfloat16
F32 = jnp.float32
MESH = pl.DeviceIdType.MESH
NT = (((1,), (1,)), ((), ()))
NN = (((1,), (0,)), ((), ()))
SCALE = HEAD_DIM**-0.5
EXP2_SCALE = SCALE * 1.4426950408889634


def dot(a, b, dims=NN):
    return lax.dot_general(a, b, dims, preferred_element_type=F32)


def left_half(rows):
    return lax.broadcasted_iota(jnp.int32, (rows, 128), 1) < HEAD_DIM


def pair(a, b):
    return jnp.concatenate([a, b], axis=1)


def fold(x, lo):
    cols = slice(lo, lo + HEAD_DIM)
    return pair(x[: ROWS // 2, cols], x[ROWS // 2 :, cols])


def probabilities(qd, kv):
    left = left_half(ROWS)
    scores = dot(jnp.where(left, qd, jnp.zeros_like(qd)), kv, NT)
    top = jnp.max(scores, axis=1, keepdims=True)
    e = jnp.exp2((scores - top) * EXP2_SCALE)
    inv = 1.0 / jnp.sum(e, axis=1, keepdims=True)
    return e.astype(BF), inv


def fresh_first(qd, kv, acc):
    left = left_half(ROWS)
    e16, inv = probabilities(qd, kv)
    a16 = (dot(e16, kv) * inv).astype(BF)
    delta = jnp.sum(
        jnp.where(left, 0.0, a16.astype(F32) * qd.astype(F32)), axis=1, keepdims=True
    )
    scaled = (qd.astype(F32) * jnp.where(left, inv * SCALE, inv)).T.astype(BF)
    acc[...] += dot(scaled[HEAD_DIM:], e16)
    return e16, fold(a16, HEAD_DIM), jnp.where(left, inv * SCALE, delta), scaled[:HEAD_DIM]


def fresh_second(qd, kv, e16, stats, q_scaled, acc):
    left = left_half(ROWS)
    dprob = dot(jnp.where(left, jnp.zeros_like(qd), qd), kv, NT)
    ds = (e16.astype(F32) * (dprob - stats[:, HEAD_DIM : HEAD_DIM + 1])).astype(BF)
    dq = dot(ds, kv) * stats[:, 0:1]
    acc[...] += dot(q_scaled, ds)
    return fold(dq.astype(BF), 0)


def stale_tile(qd, kv):
    e16, inv = probabilities(qd, kv)
    return fold((dot(e16, kv) * inv).astype(BF), HEAD_DIM)


def loop(lo, hi, fn):
    def step(n, carry):
        fn(n)
        return carry

    lax.fori_loop(lo, hi, step, 0)


def kernel(
    x_hbm, s_hbm, wq_hbm, wk_hbm, wv_hbm, wo_hbm, g_hbm,
    mixed_out, gradx_out, gv_out, go_out,
    x2, g2, s, wq, wk, wv, wo, load_sem, share_sem,
    st_kv, st_qd, st_ks,
    kv_w, qd_w, ks_w, kv_q, qd_q, ks_q,
    send_w, recv_w, send_q, recv_q,
    e_w, e_q, stats, q_scaled, acc, kmix,
    out_a, out_dq, out_t, out_dv, out_dk, part_dv, part_dk, row_a, row_dq, row_t,
    home_a, home_dq, home_t, home_dv, home_dk, home_dvp, home_dkp, sib_dv, sib_dk, pair_send, pair_recv,
    hsend, hrecv, psend, precv, asend, arecv, apsend, aprecv,
    x_t, dv2, grads, from_y, ysum, from_xz, gathered, final,
    mixed, gradx, gv, go,
    dsem, ysend, yrecv, xsend, xrecv, gsend, grecv, out_sem,
):
    img = lax.axis_index("img")
    me = lax.axis_index("patch")
    core = lax.rem(img, 2)
    zlo = lax.rem(img // 2, 2)
    yy = img // 4
    mine_e = me // 4
    shared_core = lax.rem(me // 2, 2)
    shared_img = img - core + shared_core
    holds = core == shared_core
    first_q = 4 * lax.rem(me, 2) + 2 * core
    my_helper_core = lax.rem(me, 4) // 2

    def helper(c, e):
        return img - core + my_helper_core, 4 * e + 2 * c + me // 4
    core_one = img - core + 1
    sibling = img + 1 - 2 * core

    loads = [
        pltpu.make_async_copy(src, dst, load_sem.at[n])
        for n, (src, dst) in enumerate(
            (
                (x_hbm, x2.at[core]), (wk_hbm, wk), (wv_hbm, wv), (wq_hbm, wq),
                (g_hbm, g2.at[core]), (wo_hbm, wo), (s_hbm, s),
            )
        )
    ]
    for copy in loads[:3]:
        copy.start()

    barrier = pltpu.get_barrier_semaphore()
    for off in range(1, N_PATCH):
        pl.semaphore_signal(
            barrier, inc=1, device_id=(img, lax.rem(me + off, N_PATCH)), device_id_type=MESH
        )
    for off in range(1, N_IMG):
        pl.semaphore_signal(
            barrier, inc=1, device_id=(lax.rem(img + off, N_IMG), me), device_id_type=MESH
        )
    for off in range(1, N_PATCH):
        for there in (img + 2 - 4 * zlo, sibling):
            pl.semaphore_signal(
                barrier, inc=1, device_id=(there, lax.rem(me + off, N_PATCH)), device_id_type=MESH
            )

    def turn(off, sign=1):
        dx = off % 4 if sign == 1 else 4 - off % 4
        return lax.rem(me // 4 + off // 4, 2) * 4 + lax.rem(me + dx, 4)

    def peers(fn):
        for off in (5, 1, 7, 3, 4, 6, 2):
            fn(turn(off))

    def to_whole(kind, stage, land, peer):
        return pltpu.make_async_remote_copy(
            src_ref=stage.at[peer], dst_ref=land.at[me],
            send_sem=send_w.at[kind, peer], recv_sem=recv_w.at[kind, me],
            device_id=(img, peer), device_id_type=MESH,
        )

    def from_whole(kind, land, peer):
        return pltpu.make_async_remote_copy(
            src_ref=land.at[peer], dst_ref=land.at[peer],
            send_sem=send_w.at[kind, peer], recv_sem=recv_w.at[kind, peer],
            device_id=(img, peer), device_id_type=MESH,
        )

    def to_quarter(kind, stage, land, e, n):
        peer = 4 * e + 2 * core + n
        return peer, pltpu.make_async_remote_copy(
            src_ref=stage.at[N_PATCH + e], dst_ref=land.at[me],
            send_sem=send_q.at[kind, peer], recv_sem=recv_q.at[kind, me],
            device_id=(img, peer), device_id_type=MESH,
        )

    def each_quarter(fn):
        for e in range(2):
            for n in range(2):
                fn(e, n)

    def send_quarter(kind, stage, land):
        def one(e, n):
            peer, copy = to_quarter(kind, stage, land, e, n)

            @pl.when(peer != me)
            def _():
                copy.start()

        each_quarter(one)

        @pl.when(holds)
        def _():
            land[me] = stage[N_PATCH + mine_e]

    def from_quarter(kind, land, peer):
        return pltpu.make_async_remote_copy(
            src_ref=land.at[peer], dst_ref=land.at[peer],
            send_sem=send_q.at[kind, peer], recv_sem=recv_q.at[kind, peer],
            device_id=(img, peer), device_id_type=MESH,
        )

    def hand_over(n, src, dst):
        return pltpu.make_async_remote_copy(
            src_ref=src, dst_ref=dst, send_sem=pair_send.at[n], recv_sem=pair_recv.at[n],
            device_id=(sibling, me), device_id_type=MESH,
        )

    def pass_keys(n, kind, land):
        @pl.when(holds)
        def _():
            peers(lambda peer: from_quarter(kind, land, peer).wait_recv())
            hand_over(n, land, land).start()

    def wait_keys(n, land):
        @pl.when(jnp.logical_not(holds))
        def _():
            hand_over(n, land, land).wait_recv()

    def pass_sums(n, part, arrived):
        @pl.when(jnp.logical_not(holds))
        def _():
            hand_over(n, part, arrived).start()

    def send_sums(n, kind, part, arrived, land):
        @pl.when(holds)
        def _():
            hand_over(n, part, arrived).wait_recv()
            part[...] = (part[...].astype(F32) + arrived[...].astype(F32)).astype(BF)
            peers(lambda peer: go_home(kind, part, land, peer).start())
            land[me] = part[me]

    def receive_sums(kind, land):
        def one(e, n):
            peer = 4 * e + 2 * core + n

            @pl.when(peer != me)
            def _():
                come_home(kind, land, peer).wait_recv()

        each_quarter(one)

    def quarter_rows(e):
        there, peer = helper(core, e)
        here = jnp.logical_and(there == img, peer == me)
        return here, pltpu.make_async_remote_copy(
            src_ref=st_qd.at[N_PATCH + e], dst_ref=qd_q.at[lax.rem(me, 2)],
            send_sem=send_q.at[1, e], recv_sem=recv_q.at[1, lax.rem(me, 2)],
            device_id=(there, peer), device_id_type=MESH,
        )

    def owned(t):
        return jnp.logical_and(holds, first_q + t == me)

    def quarter_rows_in(t):
        return pltpu.make_async_remote_copy(
            src_ref=qd_q.at[t], dst_ref=qd_q.at[t],
            send_sem=send_q.at[1, t], recv_sem=recv_q.at[1, t],
            device_id=(shared_img, first_q + t), device_id_type=MESH,
        )

    def share(core_from, ref, n):
        return pltpu.make_async_remote_copy(
            src_ref=ref.at[core_from], dst_ref=ref.at[core_from],
            send_sem=share_sem.at[n], recv_sem=share_sem.at[2 + n],
            device_id=(sibling, me), device_id_type=MESH,
        )

    def stage_pairs(stage, a, b):
        for h in range(HEADS):
            cols = slice(h * HEAD_DIM, (h + 1) * HEAD_DIM)
            stage[h] = pair(a[:, cols], b[:, cols])

    loads[0].wait()
    loads[1].wait()
    for copy in loads[3:]:
        copy.start()
    key = dot(x2[core], wk[...]).astype(BF)
    loads[2].wait()
    value = dot(x2[core], wv[...]).astype(BF)
    stage_pairs(st_kv, key, value)
    pl.semaphore_wait(barrier, 3 * (N_PATCH - 1) + N_IMG - 1)
    peers(lambda peer: to_whole(0, st_kv, kv_w, peer).start())
    kv_w[me] = st_kv[me]
    loads[3].wait()
    query = dot(x2[core], wq[...]).astype(BF)
    loads[4].wait()
    loads[5].wait()
    dattend = dot(g2[core], wo[...], NT).astype(BF)
    stage_pairs(st_qd, query, dattend)
    for off in range(1, N_PATCH):
        to_whole(1, st_qd, qd_w, turn(off, -1)).start()
    qd_w[me] = st_qd[me]
    send_quarter(0, st_kv, kv_q)
    for e in range(2):
        here, copy = quarter_rows(e)

        @pl.when(jnp.logical_not(here))
        def _():
            copy.start()

        @pl.when(here)
        def _():
            qd_q[lax.rem(me, 2)] = st_qd[N_PATCH + e]

    @pl.when(core == 1)
    def _():
        share(1, x2, 0).start()

    @pl.when(core == 0)
    def _():
        share(0, g2, 1).start()

    loads[6].wait()
    key_old = dot(s[...], wk[...]).astype(BF)
    value_old = dot(s[...], wv[...]).astype(BF)
    stage_pairs(st_ks, key_old, value_old)
    ks_w[me] = st_ks[me]

    @pl.when(core == 0)
    def _():
        share(1, x2, 0).wait_recv()
        x_t[:, :ROWS] = x2[0].T
        x_t[:, ROWS:] = x2[1].T

    @pl.when(core == 1)
    def _():
        share(0, g2, 1).wait_recv()

    def go_home(kind, src, land, peer):
        return pltpu.make_async_remote_copy(
            src_ref=src.at[peer], dst_ref=land.at[me],
            send_sem=hsend.at[kind, peer], recv_sem=hrecv.at[kind, me],
            device_id=(img, peer), device_id_type=MESH,
        )

    def come_home(kind, land, peer):
        return pltpu.make_async_remote_copy(
            src_ref=land.at[peer], dst_ref=land.at[peer],
            send_sem=hsend.at[kind, peer], recv_sem=hrecv.at[kind, peer],
            device_id=(img, peer), device_id_type=MESH,
        )

    def go_home_rows(kind, src, land, t):
        return pltpu.make_async_remote_copy(
            src_ref=src.at[t], dst_ref=land.at[N_PATCH + mine_e],
            send_sem=psend.at[kind, t], recv_sem=precv.at[kind, mine_e],
            device_id=(shared_img, first_q + t), device_id_type=MESH,
        )

    def come_home_rows(kind, land, e):
        there, peer = helper(core, e)
        here = jnp.logical_and(there == img, peer == me)
        return here, pltpu.make_async_remote_copy(
            src_ref=land.at[N_PATCH + e], dst_ref=land.at[N_PATCH + e],
            send_sem=psend.at[kind, e], recv_sem=precv.at[kind, e],
            device_id=(there, peer), device_id_type=MESH,
        )

    def a_home(i):
        return pltpu.make_async_remote_copy(
            src_ref=out_a.at[i], dst_ref=home_a.at[core, me],
            send_sem=asend.at[i], recv_sem=arecv.at[core, me],
            device_id=(core_one, i), device_id_type=MESH,
        )

    def a_in(c, peer):
        return pltpu.make_async_remote_copy(
            src_ref=home_a.at[c, peer], dst_ref=home_a.at[c, peer],
            send_sem=asend.at[peer], recv_sem=arecv.at[c, peer],
            device_id=(core_one, peer), device_id_type=MESH,
        )

    def a_home_rows(t):
        return pltpu.make_async_remote_copy(
            src_ref=row_a.at[t], dst_ref=home_a.at[shared_core, N_PATCH + mine_e],
            send_sem=apsend.at[t], recv_sem=aprecv.at[shared_core, mine_e],
            device_id=(core_one, first_q + t), device_id_type=MESH,
        )

    def a_in_rows(c, e):
        return pltpu.make_async_remote_copy(
            src_ref=home_a.at[c, N_PATCH + e], dst_ref=home_a.at[c, N_PATCH + e],
            send_sem=apsend.at[e], recv_sem=aprecv.at[c, e],
            device_id=helper(c, e), device_id_type=MESH,
        )

    def stays(peer):
        return jnp.logical_and(peer == me, core == 1)

    def put(out):
        for j in range(N_PATCH):
            out[j] = fold(acc[:, j * ROWS : (j + 1) * ROWS].T.astype(BF), 0)

    def clear():
        acc[...] = jnp.zeros_like(acc)

    peers(lambda peer: from_whole(0, kv_w, peer).wait_recv())
    clear()

    def first_whole(off):
        i = turn(off)

        @pl.when(off == 6)
        def _():
            pass_keys(0, 0, kv_q)

        @pl.when(i != me)
        def _():
            from_whole(1, qd_w, i).wait_recv()

        e_w[i], out_a[i], stats[i], q_scaled[i] = fresh_first(
            qd_w[i], kv_w[...].reshape(TOKENS, 128), acc
        )

        @pl.when(jnp.logical_not(stays(i)))
        def _():
            a_home(i).start()

    loop(0, N_PATCH, first_whole)

    @pl.when(core == 1)
    def _():
        home_a[1, me] = out_a[me]

    put(out_dv)
    peers(lambda peer: go_home(3, out_dv, home_dv, peer).start())
    home_dv[me] = out_dv[me]
    peers(lambda peer: to_whole(2, st_ks, ks_w, peer).start())

    wait_keys(0, kv_q)
    for t in range(2):
        @pl.when(jnp.logical_not(owned(t)))
        def _():
            quarter_rows_in(t).wait_recv()

    clear()

    def first_quarter(t):
        e_q[t], row_a[t], stats[N_PATCH + t], q_scaled[N_PATCH + t] = fresh_first(
            qd_q[t], kv_q[...].reshape(TOKENS, 128), acc
        )

    loop(0, 2, first_quarter)
    for t in range(2):
        here = stays(first_q + t)

        @pl.when(jnp.logical_not(here))
        def _():
            a_home_rows(t).start()

        @pl.when(here)
        def _():
            home_a[shared_core, N_PATCH + mine_e] = row_a[t]

    put(part_dv)
    pass_sums(2, part_dv, sib_dv)
    send_sums(2, 5, part_dv, sib_dv, home_dvp)
    send_quarter(2, st_ks, ks_q)

    def unfold(src, r):
        cols = slice(r * HEAD_DIM, (r + 1) * HEAD_DIM)
        return jnp.concatenate([src[h][:, cols] for h in range(HEADS)], axis=1)

    def add_shared(land, parts):
        for e in range(2):
            first = 4 * e + 2 * core
            total = parts[first].astype(F32) + parts[first + 1].astype(F32)
            land[N_PATCH + e] = total.astype(BF)

    def y_copy(off):
        peer = lax.rem(yy + off, 4)
        return pltpu.make_async_remote_copy(
            src_ref=grads.at[:, pl.ds(pl.multiple_of(SLOT * peer, 16), SLOT)],
            dst_ref=from_y.at[off - 1],
            send_sem=ysend.at[off - 1], recv_sem=yrecv.at[off - 1],
            device_id=(4 * peer + 2 * zlo + core, me), device_id_type=MESH,
        )

    grads[:, 800:] = jnp.zeros((N_PATCH, PART - 800, 128), BF)

    @pl.when(core == 1)
    def _():
        for c in range(2):
            for n in range(N_PATCH):
                if c == 1:
                    @pl.when(n != me)
                    def _():
                        a_in(c, n).wait_recv()
                else:
                    a_in(c, n).wait_recv()
            for e in range(2):
                there, peer = helper(c, e)

                @pl.when(jnp.logical_not(jnp.logical_and(there == img, peer == me)))
                def _():
                    a_in_rows(c, e).wait_recv()
        a_t = jnp.concatenate(
            [unfold(home_a.at[c], r).T for c in range(2) for r in range(2)], axis=1
        )
        g_all = g2[...].reshape(2 * ROWS, C)
        for q in range(N_PATCH):
            part = dot(a_t[80 * q : 80 * q + 80], g_all).astype(BF)
            for c in range(10):
                grads[q, 80 * c : 80 * c + 80] = part[:, 128 * c : 128 * c + 128]
        for off in range(1, 4):
            y_copy(off).start()

    clear()

    def second_whole(off):
        i = turn(off)
        out_dq[i] = fresh_second(
            qd_w[i], kv_w[...].reshape(TOKENS, 128), e_w[i], stats[i], q_scaled[i], acc
        )

        @pl.when(i != me)
        def _():
            go_home(0, out_dq, home_dq, i).start()

    loop(0, N_PATCH // 2, second_whole)

    peers(lambda peer: come_home(3, home_dv, peer).wait_recv())
    receive_sums(5, home_dvp)
    add_shared(home_dv, home_dvp)
    for r in range(2):
        dv2[core, r * ROWS // 2 : (r + 1) * ROWS // 2] = unfold(home_dv, r)
    dv_share = pltpu.make_async_remote_copy(
        src_ref=dv2.at[1], dst_ref=dv2.at[1], send_sem=dsem.at[0], recv_sem=dsem.at[1],
        device_id=(sibling, me), device_id_type=MESH,
    )

    @pl.when(core == 1)
    def _():
        dv_share.start()

    @pl.when(core == 0)
    def _():
        dv_share.wait_recv()
        dv_all = dv2[...].reshape(2 * ROWS, INNER)
        for q in range(N_PATCH):
            part = dot(x_t[160 * q : 160 * q + 160], dv_all).astype(BF)
            for c in range(5):
                grads[q, 160 * c : 160 * c + 160] = part[:, 128 * c : 128 * c + 128]
        for off in range(1, 4):
            y_copy(off).start()

    loop(N_PATCH // 2, N_PATCH, second_whole)
    home_dq[me] = out_dq[me]
    put(out_dk)
    peers(lambda peer: go_home(1, out_dk, home_dk, peer).start())
    home_dk[me] = out_dk[me]

    clear()

    def second_quarter(t):
        row_dq[t] = fresh_second(
            qd_q[t], kv_q[...].reshape(TOKENS, 128), e_q[t], stats[N_PATCH + t],
            q_scaled[N_PATCH + t], acc,
        )

    loop(0, 2, second_quarter)

    def send_rows(kind, src, land):
        for t in range(2):
            @pl.when(jnp.logical_not(owned(t)))
            def _():
                go_home_rows(kind, src, land, t).start()

            @pl.when(owned(t))
            def _():
                land[N_PATCH + mine_e] = src[t]

    send_rows(0, row_dq, home_dq)
    put(part_dk)
    pass_sums(3, part_dk, sib_dk)

    peers(lambda peer: from_whole(2, ks_w, peer).wait_recv())
    kmix[...] = ks_w[...]

    def stale_whole(off):
        i = turn(off)

        @pl.when(off == 2)
        def _():
            send_sums(3, 4, part_dk, sib_dk, home_dkp)

        @pl.when(off == 6)
        def _():
            pass_keys(1, 2, ks_q)

        kmix[i] = kv_w[i]
        out_t[i] = stale_tile(qd_w[i], kmix[...].reshape(TOKENS, 128))
        kmix[i] = ks_w[i]

        @pl.when(i != me)
        def _():
            go_home(2, out_t, home_t, i).start()

    loop(0, N_PATCH, stale_whole)
    home_t[me] = out_t[me]
    wait_keys(1, ks_q)
    kmix[...] = ks_q[...]

    def stale_quarter(t):
        i = first_q + t
        kmix[i] = kv_q[i]
        row_t[t] = stale_tile(qd_q[t], kmix[...].reshape(TOKENS, 128))
        kmix[i] = ks_q[i]

    loop(0, 2, stale_quarter)
    send_rows(1, row_t, home_t)

    for off in range(1, 4):
        y_copy(off).wait_recv()

    def y_add(q):
        total = grads[q, pl.ds(pl.multiple_of(SLOT * yy, 16), SLOT)].astype(F32)
        for n in range(3):
            total = total + from_y[n, q].astype(F32)
        ysum[q, :SLOT] = total.astype(BF)
        ysum[q, SLOT:] = jnp.zeros((2 * HALF - SLOT, 128), BF)

    loop(0, N_PATCH, y_add)
    plane = zlo * N_PATCH + me

    def xz_peer(off):
        there = lax.rem(plane + off, 16)
        return there, there // N_PATCH, lax.rem(there, N_PATCH)

    def xz_send(off):
        there, z_there, p_there = xz_peer(off)
        return pltpu.make_async_remote_copy(
            src_ref=ysum.at[p_there, pl.ds(pl.multiple_of(HALF * z_there, 16), HALF)],
            dst_ref=from_xz.at[plane],
            send_sem=xsend.at[there], recv_sem=xrecv.at[plane],
            device_id=(4 * yy + 2 * z_there + core, p_there), device_id_type=MESH,
        )

    def xz_recv(off):
        there, z_there, p_there = xz_peer(off)
        return pltpu.make_async_remote_copy(
            src_ref=from_xz.at[there], dst_ref=from_xz.at[there],
            send_sem=xsend.at[there], recv_sem=xrecv.at[there],
            device_id=(4 * yy + 2 * z_there + core, p_there), device_id_type=MESH,
        )

    loop(1, 16, lambda off: xz_send(off).start())
    from_xz[plane] = ysum[me, pl.ds(pl.multiple_of(HALF * zlo, 16), HALF)]

    def receive_rows(kind, land):
        for e in range(2):
            here, copy = come_home_rows(kind, land, e)

            @pl.when(jnp.logical_not(here))
            def _():
                copy.wait_recv()

    peers(lambda peer: come_home(0, home_dq, peer).wait_recv())
    receive_rows(0, home_dq)
    peers(lambda peer: come_home(1, home_dk, peer).wait_recv())
    receive_sums(4, home_dkp)
    add_shared(home_dk, home_dkp)
    dquery = jnp.concatenate([unfold(home_dq, 0), unfold(home_dq, 1)], axis=0)
    dkey = jnp.concatenate([unfold(home_dk, 0), unfold(home_dk, 1)], axis=0)
    gradx[...] = (
        dot(dquery, wq[...], NT) + dot(dkey, wk[...], NT) + dot(dv2[core], wv[...], NT)
    ).astype(BF)
    gradx_copy = pltpu.make_async_copy(gradx, gradx_out.at[0], out_sem.at[0])
    gradx_copy.start()

    loop(1, 16, lambda off: xz_recv(off).wait_recv())
    total = from_xz[0].astype(F32)
    for n in range(1, 16):
        total = total + from_xz[n].astype(F32)
    gathered[img] = total.astype(BF)

    def gather_send(off):
        peer = lax.rem(img + off, N_IMG)
        return pltpu.make_async_remote_copy(
            src_ref=gathered.at[img], dst_ref=gathered.at[img],
            send_sem=gsend.at[peer], recv_sem=grecv.at[img],
            device_id=(peer, me), device_id_type=MESH,
        )

    def gather_recv(off):
        peer = lax.rem(img + off, N_IMG)
        return pltpu.make_async_remote_copy(
            src_ref=gathered.at[peer], dst_ref=gathered.at[peer],
            send_sem=gsend.at[peer], recv_sem=grecv.at[peer],
            device_id=(peer, me), device_id_type=MESH,
        )

    loop(1, N_IMG, lambda off: gather_send(off).start())

    peers(lambda peer: come_home(2, home_t, peer).wait_recv())
    receive_rows(1, home_t)
    for r in range(2):
        mixed[r * ROWS // 2 : (r + 1) * ROWS // 2] = dot(unfold(home_t, r), wo[...]).astype(BF)
    mixed_copy = pltpu.make_async_copy(mixed, mixed_out.at[0], out_sem.at[1])
    mixed_copy.start()

    loop(1, N_IMG, lambda off: gather_recv(off).wait_recv())
    for kind in range(2):
        for n in range(4):
            final[kind, SLOT * n : SLOT * n + HALF] = gathered[4 * n + kind].astype(F32)
            final[kind, SLOT * n + HALF : SLOT * (n + 1)] = gathered[4 * n + 2 + kind][
                : SLOT - HALF
            ].astype(F32)
    for c in range(5):
        gv[:, 128 * c : 128 * c + 128] = final[0, 160 * c : 160 * c + 160]
    for c in range(10):
        go[:, 128 * c : 128 * c + 128] = final[1, 80 * c : 80 * c + 80]
    gv_copy = pltpu.make_async_copy(gv, gv_out, out_sem.at[2])
    go_copy = pltpu.make_async_copy(go, go_out, out_sem.at[3])
    gv_copy.start()
    go_copy.start()

    for kind, stage, land in ((0, st_kv, kv_w), (1, st_qd, qd_w), (2, st_ks, ks_w)):
        peers(lambda peer: to_whole(kind, stage, land, peer).wait_send())
    for kind, stage, land in ((0, st_kv, kv_q), (2, st_ks, ks_q)):
        def sent(e, n):
            peer, copy = to_quarter(kind, stage, land, e, n)

            @pl.when(peer != me)
            def _():
                copy.wait_send()

        each_quarter(sent)

    for e in range(2):
        here, copy = quarter_rows(e)

        @pl.when(jnp.logical_not(here))
        def _():
            copy.wait_send()

    @pl.when(holds)
    def _():
        hand_over(0, kv_q, kv_q).wait_send()
        hand_over(1, ks_q, ks_q).wait_send()
        peers(lambda peer: go_home(4, part_dk, home_dkp, peer).wait_send())
        peers(lambda peer: go_home(5, part_dv, home_dvp, peer).wait_send())

    @pl.when(jnp.logical_not(holds))
    def _():
        hand_over(2, part_dv, sib_dv).wait_send()
        hand_over(3, part_dk, sib_dk).wait_send()

    @pl.when(core == 1)
    def _():
        share(1, x2, 0).wait_send()
        dv_share.wait_send()

    @pl.when(core == 0)
    def _():
        share(0, g2, 1).wait_send()

    for kind, src, land in (
        (0, out_dq, home_dq), (1, out_dk, home_dk), (2, out_t, home_t),
        (3, out_dv, home_dv),
    ):
        peers(lambda peer: go_home(kind, src, land, peer).wait_send())
    for kind, src, land in ((0, row_dq, home_dq), (1, row_t, home_t)):
        for t in range(2):
            @pl.when(jnp.logical_not(owned(t)))
            def _():
                go_home_rows(kind, src, land, t).wait_send()

    for n in range(N_PATCH):
        @pl.when(jnp.logical_not(stays(n)))
        def _():
            a_home(n).wait_send()

    for t in range(2):
        @pl.when(jnp.logical_not(stays(first_q + t)))
        def _():
            a_home_rows(t).wait_send()

    for off in range(1, 4):
        y_copy(off).wait_send()
    loop(1, 16, lambda off: xz_send(off).wait_send())
    loop(1, N_IMG, lambda off: gather_send(off).wait_send())
    for copy in (gradx_copy, mixed_copy, gv_copy, go_copy):
        copy.wait()


def pass_on(*refs):
    sources, results, held = refs[:4], refs[4:8], refs[8:12]
    load_sem, store_sem = refs[12:]
    loads = [pltpu.make_async_copy(sources[n], held[n], load_sem.at[n]) for n in range(4)]
    stores = [pltpu.make_async_copy(held[n], results[n], store_sem.at[n]) for n in range(4)]
    for copy in loads:
        copy.start()
    for load, store in zip(loads, stores):
        load.wait()
        store.start()
    for store in stores:
        store.wait()


def vm(*shape, dtype=BF):
    return pltpu.VMEM(shape, dtype)


def dma(*shape):
    return pltpu.SemaphoreType.DMA(shape)


def on_device(latents_now, latents_stale, w_query, w_key, w_value, w_out, cotangent):
    half = ROWS // 2
    shapes = (
        jax.ShapeDtypeStruct((1, ROWS, C), BF),
        jax.ShapeDtypeStruct((1, ROWS, C), BF),
        jax.ShapeDtypeStruct((C // N_PATCH, INNER), F32),
        jax.ShapeDtypeStruct((INNER // N_PATCH, C), F32),
    )
    anywhere = pl.BlockSpec(memory_space=pl.ANY)
    results = pl.pallas_call(
        kernel,
        out_shape=shapes,
        in_specs=[anywhere] * 7,
        out_specs=[anywhere] * 4,
        scratch_shapes=[
            vm(2, ROWS, C), vm(2, ROWS, C), vm(ROWS, C), vm(C, INNER), vm(C, INNER), vm(C, INNER), vm(INNER, C),
            dma(7), dma(4),
            vm(10, ROWS, 128), vm(10, ROWS, 128), vm(10, ROWS, 128),
            vm(8, ROWS, 128), vm(8, ROWS, 128), vm(8, ROWS, 128),
            vm(8, ROWS, 128), vm(2, ROWS, 128), vm(8, ROWS, 128),
            dma(3, 8), dma(3, 8), dma(3, 8), dma(3, 8),
            vm(8, ROWS, TOKENS), vm(2, ROWS, TOKENS), vm(10, ROWS, 128, dtype=F32), vm(10, HEAD_DIM, ROWS),
            vm(HEAD_DIM, TOKENS, dtype=F32), vm(8, ROWS, 128),
            vm(8, half, 128), vm(8, half, 128), vm(8, half, 128), vm(8, half, 128), vm(8, half, 128),
            vm(8, half, 128), vm(8, half, 128), vm(2, half, 128), vm(2, half, 128), vm(2, half, 128),
            vm(2, 10, half, 128), vm(10, half, 128), vm(10, half, 128), vm(10, half, 128), vm(10, half, 128),
            vm(8, half, 128), vm(8, half, 128), vm(8, half, 128), vm(8, half, 128), dma(4), dma(4),
            dma(6, 8), dma(6, 8), dma(2, 2), dma(2, 2), dma(8), dma(2, 8), dma(2), dma(2, 2),
            vm(C, 2 * ROWS), vm(2, ROWS, INNER), vm(8, PART, 128), vm(3, 8, SLOT, 128), vm(8, 2 * HALF, 128),
            vm(16, HALF, 128), vm(16, HALF, 128), vm(2, PART, 128, dtype=F32),
            vm(ROWS, C), vm(ROWS, C), vm(C // N_PATCH, INNER, dtype=F32), vm(INNER // N_PATCH, C, dtype=F32),
            dma(2), dma(3), dma(3), dma(16), dma(16), dma(16), dma(16), dma(4),
        ],
        compiler_params=pltpu.CompilerParams(
            collective_id=0, has_side_effects=True, vmem_limit_bytes=56 * 2**20
        ),
        cost_estimate=pl.CostEstimate(flops=10**10, bytes_accessed=12 * 2**20, transcendentals=10**7),
    )(latents_now[0], latents_stale[0], w_query, w_key, w_value, w_out, cotangent[0])
    return pl.pallas_call(
        pass_on,
        out_shape=shapes,
        in_specs=[anywhere] * 4,
        out_specs=[anywhere] * 4,
        scratch_shapes=[pltpu.VMEM(shape.shape, shape.dtype) for shape in shapes] + [dma(4), dma(4)],
        compiler_params=pltpu.CompilerParams(vmem_limit_bytes=56 * 2**20),
        cost_estimate=pl.CostEstimate(flops=0, bytes_accessed=2 * 2**20, transcendentals=0),
    )(*results)


def solution(mesh):
    rows = P("img", "patch", None)
    return jax.shard_map(
        on_device,
        mesh=mesh,
        in_specs=(rows, rows, P(), P(), P(), P(), rows),
        out_specs=(rows, rows, P("patch", None), P("patch", None)),
        check_vma=False,
    )
```

```python
import jax
import jax.numpy as jnp
from jax import lax
from jax.experimental import pallas as pl
from jax.experimental.pallas import tpu as pltpu
from jax.sharding import PartitionSpec as P

HEADS = 10
HEAD_DIM = 64
N_PATCH = 8
N_IMG = 16
ROWS = 256
TOKENS = 2048
C = 1280
INNER = 640
PART = 832
SLOT = 208
HALF = 112
BF = jnp.bfloat16
F32 = jnp.float32
MESH = pl.DeviceIdType.MESH
NT = (((1,), (1,)), ((), ()))
NN = (((1,), (0,)), ((), ()))
SCALE = HEAD_DIM**-0.5
EXP2_SCALE = SCALE * 1.4426950408889634


def dot(a, b, dims=NN):
    return lax.dot_general(a, b, dims, preferred_element_type=F32)


def left_half(rows):
    return lax.broadcasted_iota(jnp.int32, (rows, 128), 1) < HEAD_DIM


def pair(a, b):
    return jnp.concatenate([a, b], axis=1)


def fold(x, lo):
    cols = slice(lo, lo + HEAD_DIM)
    return pair(x[: ROWS // 2, cols], x[ROWS // 2 :, cols])


def probabilities(qd, kv):
    left = left_half(ROWS)
    scores = dot(jnp.where(left, qd, jnp.zeros_like(qd)), kv, NT)
    top = jnp.max(scores, axis=1, keepdims=True)
    e = jnp.exp2((scores - top) * EXP2_SCALE)
    inv = 1.0 / jnp.sum(e, axis=1, keepdims=True)
    return e.astype(BF), inv


def both(parts, axis):
    return jnp.concatenate(parts, axis=axis)


def fresh_first(blocks, kv, acc):
    left = left_half(ROWS)
    outs, terms, rows = [], [], []
    for qd in blocks:
        e16, inv = probabilities(qd, kv)
        a16 = (dot(e16, kv) * inv).astype(BF)
        delta = jnp.sum(
            jnp.where(left, 0.0, a16.astype(F32) * qd.astype(F32)), axis=1, keepdims=True
        )
        scaled = (qd.astype(F32) * jnp.where(left, inv * SCALE, inv)).T.astype(BF)
        outs.append((e16, fold(a16, HEAD_DIM), jnp.where(left, inv * SCALE, delta), scaled[:HEAD_DIM]))
        terms.append(e16)
        rows.append(scaled[HEAD_DIM:])
    acc[...] += dot(both(rows, 1), both(terms, 0))
    return outs


def fresh_second(blocks, kv, es, stats, q_scaled, acc):
    left = left_half(ROWS)
    outs, terms = [], []
    for qd, e16, row in zip(blocks, es, stats):
        dprob = dot(jnp.where(left, jnp.zeros_like(qd), qd), kv, NT)
        ds = (e16.astype(F32) * (dprob - row[:, HEAD_DIM : HEAD_DIM + 1])).astype(BF)
        outs.append(fold((dot(ds, kv) * row[:, 0:1]).astype(BF), 0))
        terms.append(ds)
    acc[...] += dot(both(q_scaled, 1), both(terms, 0))
    return outs


def stale_tile(qd, kv):
    e16, inv = probabilities(qd, kv)
    return fold((dot(e16, kv) * inv).astype(BF), HEAD_DIM)


def loop(lo, hi, fn):
    def step(n, carry):
        fn(n)
        return carry

    lax.fori_loop(lo, hi, step, 0)


def kernel(
    x_hbm, s_hbm, wq_hbm, wk_hbm, wv_hbm, wo_hbm, g_hbm,
    mixed_out, gradx_out, gv_out, go_out,
    x2, g2, s, wq, wk, wv, wo, load_sem, share_sem,
    st_kv, st_qd, st_ks,
    kv_w, qd_w, ks_w, kv_q, qd_q, ks_q,
    send_w, recv_w, send_q, recv_q,
    e_w, e_q, stats, q_scaled, acc, kmix,
    out_a, out_dq, out_t, out_dv, out_dk, part_dv, part_dk, row_a, row_dq, row_t,
    home_a, home_dq, home_t, home_dv, home_dk, home_dvp, home_dkp, sib_dv, sib_dk, pair_send, pair_recv,
    hsend, hrecv, psend, precv, asend, arecv, apsend, aprecv,
    x_t, dv2, grads, from_y, ysum, from_xz, gathered, final,
    mixed, gradx, gv, go,
    dsem, ysend, yrecv, xsend, xrecv, gsend, grecv, out_sem,
):
    img = lax.axis_index("img")
    me = lax.axis_index("patch")
    core = lax.rem(img, 2)
    zlo = lax.rem(img // 2, 2)
    yy = img // 4
    mine_e = me // 4
    shared_core = lax.rem(me // 2, 2)
    shared_img = img - core + shared_core
    holds = core == shared_core
    first_q = 4 * lax.rem(me, 2) + 2 * core
    my_helper_core = lax.rem(me, 4) // 2

    def helper(c, e):
        return img - core + my_helper_core, 4 * e + 2 * c + me // 4
    core_one = img - core + 1
    sibling = img + 1 - 2 * core

    loads = [
        pltpu.make_async_copy(src, dst, load_sem.at[n])
        for n, (src, dst) in enumerate(
            (
                (x_hbm, x2.at[core]), (wk_hbm, wk), (wv_hbm, wv), (wq_hbm, wq),
                (g_hbm, g2.at[core]), (wo_hbm, wo), (s_hbm, s),
            )
        )
    ]
    for copy in loads[:3]:
        copy.start()

    barrier = pltpu.get_barrier_semaphore()
    for off in range(1, N_PATCH):
        pl.semaphore_signal(
            barrier, inc=1, device_id=(img, lax.rem(me + off, N_PATCH)), device_id_type=MESH
        )
    for off in range(1, N_IMG):
        pl.semaphore_signal(
            barrier, inc=1, device_id=(lax.rem(img + off, N_IMG), me), device_id_type=MESH
        )
    for off in range(1, N_PATCH):
        for there in (img + 2 - 4 * zlo, sibling):
            pl.semaphore_signal(
                barrier, inc=1, device_id=(there, lax.rem(me + off, N_PATCH)), device_id_type=MESH
            )

    def turn(off, sign=1):
        dx = off % 4 if sign == 1 else 4 - off % 4
        return lax.rem(me // 4 + off // 4, 2) * 4 + lax.rem(me + dx, 4)

    def peers(fn):
        for off in (5, 1, 7, 3, 4, 6, 2):
            fn(turn(off))

    def to_whole(kind, stage, land, peer):
        return pltpu.make_async_remote_copy(
            src_ref=stage.at[peer], dst_ref=land.at[me],
            send_sem=send_w.at[kind, peer], recv_sem=recv_w.at[kind, me],
            device_id=(img, peer), device_id_type=MESH,
        )

    def from_whole(kind, land, peer):
        return pltpu.make_async_remote_copy(
            src_ref=land.at[peer], dst_ref=land.at[peer],
            send_sem=send_w.at[kind, peer], recv_sem=recv_w.at[kind, peer],
            device_id=(img, peer), device_id_type=MESH,
        )

    def to_quarter(kind, stage, land, e, n):
        peer = 4 * e + 2 * core + n
        return peer, pltpu.make_async_remote_copy(
            src_ref=stage.at[N_PATCH + e], dst_ref=land.at[me],
            send_sem=send_q.at[kind, peer], recv_sem=recv_q.at[kind, me],
            device_id=(img, peer), device_id_type=MESH,
        )

    def each_quarter(fn):
        for e in range(2):
            for n in range(2):
                fn(e, n)

    def send_quarter(kind, stage, land):
        def one(e, n):
            peer, copy = to_quarter(kind, stage, land, e, n)

            @pl.when(peer != me)
            def _():
                copy.start()

        each_quarter(one)

        @pl.when(holds)
        def _():
            land[me] = stage[N_PATCH + mine_e]

    def from_quarter(kind, land, peer):
        return pltpu.make_async_remote_copy(
            src_ref=land.at[peer], dst_ref=land.at[peer],
            send_sem=send_q.at[kind, peer], recv_sem=recv_q.at[kind, peer],
            device_id=(img, peer), device_id_type=MESH,
        )

    def hand_over(n, src, dst):
        return pltpu.make_async_remote_copy(
            src_ref=src, dst_ref=dst, send_sem=pair_send.at[n], recv_sem=pair_recv.at[n],
            device_id=(sibling, me), device_id_type=MESH,
        )

    def pass_keys(n, kind, land):
        @pl.when(holds)
        def _():
            peers(lambda peer: from_quarter(kind, land, peer).wait_recv())
            hand_over(n, land, land).start()

    def wait_keys(n, land):
        @pl.when(jnp.logical_not(holds))
        def _():
            hand_over(n, land, land).wait_recv()

    def pass_sums(n, part, arrived):
        @pl.when(jnp.logical_not(holds))
        def _():
            hand_over(n, part, arrived).start()

    def send_sums(n, kind, part, arrived, land):
        @pl.when(holds)
        def _():
            hand_over(n, part, arrived).wait_recv()
            part[...] = (part[...].astype(F32) + arrived[...].astype(F32)).astype(BF)
            peers(lambda peer: go_home(kind, part, land, peer).start())
            land[me] = part[me]

    def receive_sums(kind, land):
        def one(e, n):
            peer = 4 * e + 2 * core + n

            @pl.when(peer != me)
            def _():
                come_home(kind, land, peer).wait_recv()

        each_quarter(one)

    def quarter_rows(e):
        there, peer = helper(core, e)
        here = jnp.logical_and(there == img, peer == me)
        return here, pltpu.make_async_remote_copy(
            src_ref=st_qd.at[N_PATCH + e], dst_ref=qd_q.at[lax.rem(me, 2)],
            send_sem=send_q.at[1, e], recv_sem=recv_q.at[1, lax.rem(me, 2)],
            device_id=(there, peer), device_id_type=MESH,
        )

    def owned(t):
        return jnp.logical_and(holds, first_q + t == me)

    def quarter_rows_in(t):
        return pltpu.make_async_remote_copy(
            src_ref=qd_q.at[t], dst_ref=qd_q.at[t],
            send_sem=send_q.at[1, t], recv_sem=recv_q.at[1, t],
            device_id=(shared_img, first_q + t), device_id_type=MESH,
        )

    def share(core_from, ref, n):
        return pltpu.make_async_remote_copy(
            src_ref=ref.at[core_from], dst_ref=ref.at[core_from],
            send_sem=share_sem.at[n], recv_sem=share_sem.at[2 + n],
            device_id=(sibling, me), device_id_type=MESH,
        )

    def stage_pairs(stage, a, b):
        for h in range(HEADS):
            cols = slice(h * HEAD_DIM, (h + 1) * HEAD_DIM)
            stage[h] = pair(a[:, cols], b[:, cols])

    loads[0].wait()
    loads[1].wait()
    for copy in loads[3:]:
        copy.start()
    key = dot(x2[core], wk[...]).astype(BF)
    loads[2].wait()
    value = dot(x2[core], wv[...]).astype(BF)
    stage_pairs(st_kv, key, value)
    pl.semaphore_wait(barrier, 3 * (N_PATCH - 1) + N_IMG - 1)
    peers(lambda peer: to_whole(0, st_kv, kv_w, peer).start())
    kv_w[me] = st_kv[me]
    loads[3].wait()
    query = dot(x2[core], wq[...]).astype(BF)
    loads[4].wait()
    loads[5].wait()
    dattend = dot(g2[core], wo[...], NT).astype(BF)
    stage_pairs(st_qd, query, dattend)
    for off in range(1, N_PATCH):
        to_whole(1, st_qd, qd_w, turn(off, -1)).start()
    qd_w[me] = st_qd[me]
    send_quarter(0, st_kv, kv_q)
    for e in range(2):
        here, copy = quarter_rows(e)

        @pl.when(jnp.logical_not(here))
        def _():
            copy.start()

        @pl.when(here)
        def _():
            qd_q[lax.rem(me, 2)] = st_qd[N_PATCH + e]

    @pl.when(core == 1)
    def _():
        share(1, x2, 0).start()

    @pl.when(core == 0)
    def _():
        share(0, g2, 1).start()

    loads[6].wait()
    key_old = dot(s[...], wk[...]).astype(BF)
    value_old = dot(s[...], wv[...]).astype(BF)
    stage_pairs(st_ks, key_old, value_old)
    ks_w[me] = st_ks[me]

    @pl.when(core == 0)
    def _():
        share(1, x2, 0).wait_recv()
        x_t[:, :ROWS] = x2[0].T
        x_t[:, ROWS:] = x2[1].T

    @pl.when(core == 1)
    def _():
        share(0, g2, 1).wait_recv()

    def go_home(kind, src, land, peer):
        return pltpu.make_async_remote_copy(
            src_ref=src.at[peer], dst_ref=land.at[me],
            send_sem=hsend.at[kind, peer], recv_sem=hrecv.at[kind, me],
            device_id=(img, peer), device_id_type=MESH,
        )

    def come_home(kind, land, peer):
        return pltpu.make_async_remote_copy(
            src_ref=land.at[peer], dst_ref=land.at[peer],
            send_sem=hsend.at[kind, peer], recv_sem=hrecv.at[kind, peer],
            device_id=(img, peer), device_id_type=MESH,
        )

    def go_home_rows(kind, src, land, t):
        return pltpu.make_async_remote_copy(
            src_ref=src.at[t], dst_ref=land.at[N_PATCH + mine_e],
            send_sem=psend.at[kind, t], recv_sem=precv.at[kind, mine_e],
            device_id=(shared_img, first_q + t), device_id_type=MESH,
        )

    def come_home_rows(kind, land, e):
        there, peer = helper(core, e)
        here = jnp.logical_and(there == img, peer == me)
        return here, pltpu.make_async_remote_copy(
            src_ref=land.at[N_PATCH + e], dst_ref=land.at[N_PATCH + e],
            send_sem=psend.at[kind, e], recv_sem=precv.at[kind, e],
            device_id=(there, peer), device_id_type=MESH,
        )

    def a_home(i):
        return pltpu.make_async_remote_copy(
            src_ref=out_a.at[i], dst_ref=home_a.at[core, me],
            send_sem=asend.at[i], recv_sem=arecv.at[core, me],
            device_id=(core_one, i), device_id_type=MESH,
        )

    def a_in(c, peer):
        return pltpu.make_async_remote_copy(
            src_ref=home_a.at[c, peer], dst_ref=home_a.at[c, peer],
            send_sem=asend.at[peer], recv_sem=arecv.at[c, peer],
            device_id=(core_one, peer), device_id_type=MESH,
        )

    def a_home_rows(t):
        return pltpu.make_async_remote_copy(
            src_ref=row_a.at[t], dst_ref=home_a.at[shared_core, N_PATCH + mine_e],
            send_sem=apsend.at[t], recv_sem=aprecv.at[shared_core, mine_e],
            device_id=(core_one, first_q + t), device_id_type=MESH,
        )

    def a_in_rows(c, e):
        return pltpu.make_async_remote_copy(
            src_ref=home_a.at[c, N_PATCH + e], dst_ref=home_a.at[c, N_PATCH + e],
            send_sem=apsend.at[e], recv_sem=aprecv.at[c, e],
            device_id=helper(c, e), device_id_type=MESH,
        )

    def stays(peer):
        return jnp.logical_and(peer == me, core == 1)

    def put(out):
        for j in range(N_PATCH):
            out[j] = fold(acc[:, j * ROWS : (j + 1) * ROWS].T.astype(BF), 0)

    def clear():
        acc[...] = jnp.zeros_like(acc)

    peers(lambda peer: from_whole(0, kv_w, peer).wait_recv())
    clear()

    def first_pair(i, qd, kv, e, a):
        outs = fresh_first([qd[n] for n in i[0]], kv[...].reshape(TOKENS, 128), acc)
        for n, at, out in zip(*i, outs):
            e[n], a[n], stats[at], q_scaled[at] = out

    def two(k):
        return turn(2 * k), turn(2 * k + 1)

    def first_whole(k):
        i = two(k)

        @pl.when(k == 3)
        def _():
            pass_keys(0, 0, kv_q)

        for n in i:
            @pl.when(n != me)
            def _():
                from_whole(1, qd_w, n).wait_recv()

        first_pair((i, i), qd_w, kv_w, e_w, out_a)
        for n in i:
            @pl.when(jnp.logical_not(stays(n)))
            def _():
                a_home(n).start()

    loop(0, 4, first_whole)

    @pl.when(core == 1)
    def _():
        home_a[1, me] = out_a[me]

    put(out_dv)
    peers(lambda peer: go_home(3, out_dv, home_dv, peer).start())
    home_dv[me] = out_dv[me]
    peers(lambda peer: to_whole(2, st_ks, ks_w, peer).start())

    wait_keys(0, kv_q)
    for t in range(2):
        @pl.when(jnp.logical_not(owned(t)))
        def _():
            quarter_rows_in(t).wait_recv()

    clear()

    first_pair(((0, 1), (N_PATCH, N_PATCH + 1)), qd_q, kv_q, e_q, row_a)
    for t in range(2):
        here = stays(first_q + t)

        @pl.when(jnp.logical_not(here))
        def _():
            a_home_rows(t).start()

        @pl.when(here)
        def _():
            home_a[shared_core, N_PATCH + mine_e] = row_a[t]

    put(part_dv)
    pass_sums(2, part_dv, sib_dv)
    send_sums(2, 5, part_dv, sib_dv, home_dvp)
    send_quarter(2, st_ks, ks_q)

    def unfold(src, r):
        cols = slice(r * HEAD_DIM, (r + 1) * HEAD_DIM)
        return jnp.concatenate([src[h][:, cols] for h in range(HEADS)], axis=1)

    def add_shared(land, parts):
        for e in range(2):
            first = 4 * e + 2 * core
            total = parts[first].astype(F32) + parts[first + 1].astype(F32)
            land[N_PATCH + e] = total.astype(BF)

    def y_copy(off):
        peer = lax.rem(yy + off, 4)
        return pltpu.make_async_remote_copy(
            src_ref=grads.at[:, pl.ds(pl.multiple_of(SLOT * peer, 16), SLOT)],
            dst_ref=from_y.at[off - 1],
            send_sem=ysend.at[off - 1], recv_sem=yrecv.at[off - 1],
            device_id=(4 * peer + 2 * zlo + core, me), device_id_type=MESH,
        )

    grads[:, 800:] = jnp.zeros((N_PATCH, PART - 800, 128), BF)

    def make_grad_out():
        @pl.when(core == 1)
        def _():
            for c in range(2):
                for n in range(N_PATCH):
                    if c == 1:
                        @pl.when(n != me)
                        def _():
                            a_in(c, n).wait_recv()
                    else:
                        a_in(c, n).wait_recv()
                for e in range(2):
                    there, peer = helper(c, e)

                    @pl.when(jnp.logical_not(jnp.logical_and(there == img, peer == me)))
                    def _():
                        a_in_rows(c, e).wait_recv()
            a_t = jnp.concatenate(
                [unfold(home_a.at[c], r).T for c in range(2) for r in range(2)], axis=1
            )
            g_all = g2[...].reshape(2 * ROWS, C)
            for q in range(N_PATCH):
                part = dot(a_t[80 * q : 80 * q + 80], g_all).astype(BF)
                for c in range(10):
                    grads[q, 80 * c : 80 * c + 80] = part[:, 128 * c : 128 * c + 128]
            for off in range(1, 4):
                y_copy(off).start()

    dv_share = pltpu.make_async_remote_copy(
        src_ref=dv2.at[1], dst_ref=dv2.at[1], send_sem=dsem.at[0], recv_sem=dsem.at[1],
        device_id=(sibling, me), device_id_type=MESH,
    )

    def make_grad_value():

        peers(lambda peer: come_home(3, home_dv, peer).wait_recv())
        receive_sums(5, home_dvp)
        add_shared(home_dv, home_dvp)
        for r in range(2):
            dv2[core, r * ROWS // 2 : (r + 1) * ROWS // 2] = unfold(home_dv, r)
        @pl.when(core == 1)
        def _():
            dv_share.start()

        @pl.when(core == 0)
        def _():
            dv_share.wait_recv()
            dv_all = dv2[...].reshape(2 * ROWS, INNER)
            for q in range(N_PATCH):
                part = dot(x_t[160 * q : 160 * q + 160], dv_all).astype(BF)
                for c in range(5):
                    grads[q, 160 * c : 160 * c + 160] = part[:, 128 * c : 128 * c + 128]
            for off in range(1, 4):
                y_copy(off).start()

    clear()

    def second_pair(i, qd, kv, e, out):
        dqs = fresh_second(
            [qd[n] for n in i[0]], kv[...].reshape(TOKENS, 128), [e[n] for n in i[0]],
            [stats[n] for n in i[1]], [q_scaled[n] for n in i[1]], acc,
        )
        for n, dq in zip(i[0], dqs):
            out[n] = dq

    def second_whole(k):
        i = two(k)

        @pl.when(k == 1)
        def _():
            make_grad_out()

        @pl.when(k == 3)
        def _():
            make_grad_value()

        second_pair((i, i), qd_w, kv_w, e_w, out_dq)
        for n in i:
            @pl.when(n != me)
            def _():
                go_home(0, out_dq, home_dq, n).start()

    loop(0, 4, second_whole)
    home_dq[me] = out_dq[me]
    put(out_dk)
    peers(lambda peer: go_home(1, out_dk, home_dk, peer).start())
    home_dk[me] = out_dk[me]

    clear()

    second_pair(((0, 1), (N_PATCH, N_PATCH + 1)), qd_q, kv_q, e_q, row_dq)

    def send_rows(kind, src, land):
        for t in range(2):
            @pl.when(jnp.logical_not(owned(t)))
            def _():
                go_home_rows(kind, src, land, t).start()

            @pl.when(owned(t))
            def _():
                land[N_PATCH + mine_e] = src[t]

    send_rows(0, row_dq, home_dq)
    put(part_dk)
    pass_sums(3, part_dk, sib_dk)

    plane = zlo * N_PATCH + me

    def xz_peer(off):
        there = lax.rem(plane + off, 16)
        return there, there // N_PATCH, lax.rem(there, N_PATCH)

    def xz_send(off):
        there, z_there, p_there = xz_peer(off)
        return pltpu.make_async_remote_copy(
            src_ref=ysum.at[p_there, pl.ds(pl.multiple_of(HALF * z_there, 16), HALF)],
            dst_ref=from_xz.at[plane],
            send_sem=xsend.at[there], recv_sem=xrecv.at[plane],
            device_id=(4 * yy + 2 * z_there + core, p_there), device_id_type=MESH,
        )

    def xz_recv(off):
        there, z_there, p_there = xz_peer(off)
        return pltpu.make_async_remote_copy(
            src_ref=from_xz.at[there], dst_ref=from_xz.at[there],
            send_sem=xsend.at[there], recv_sem=xrecv.at[there],
            device_id=(4 * yy + 2 * z_there + core, p_there), device_id_type=MESH,
        )

    def sum_over_y():
        for off in range(1, 4):
            y_copy(off).wait_recv()

        def y_add(q):
            total = grads[q, pl.ds(pl.multiple_of(SLOT * yy, 16), SLOT)].astype(F32)
            for n in range(3):
                total = total + from_y[n, q].astype(F32)
            ysum[q, :SLOT] = total.astype(BF)
            ysum[q, SLOT:] = jnp.zeros((2 * HALF - SLOT, 128), BF)

        loop(0, N_PATCH, y_add)
        loop(1, 16, lambda off: xz_send(off).start())
        from_xz[plane] = ysum[me, pl.ds(pl.multiple_of(HALF * zlo, 16), HALF)]

    peers(lambda peer: from_whole(2, ks_w, peer).wait_recv())
    kmix[0] = ks_w[...]
    kmix[1] = ks_w[...]

    def stale_pair(at, i, qd, kv, ks, out):
        for t in range(2):
            kmix[t, i[t]] = kv[i[t]]
        outs = [stale_tile(qd[at[t]], kmix[t].reshape(TOKENS, 128)) for t in range(2)]
        for t in range(2):
            out[at[t]] = outs[t]
            kmix[t, i[t]] = ks[i[t]]

    def stale_whole(k):
        i = two(k)

        @pl.when(k == 3)
        def _():
            sum_over_y()

        @pl.when(k == 1)
        def _():
            send_sums(3, 4, part_dk, sib_dk, home_dkp)

        @pl.when(k == 3)
        def _():
            pass_keys(1, 2, ks_q)

        stale_pair(i, i, qd_w, kv_w, ks_w, out_t)
        for n in i:
            @pl.when(n != me)
            def _():
                go_home(2, out_t, home_t, n).start()

    loop(0, 4, stale_whole)
    home_t[me] = out_t[me]
    wait_keys(1, ks_q)
    kmix[0] = ks_q[...]
    kmix[1] = ks_q[...]

    stale_pair((0, 1), (first_q, first_q + 1), qd_q, kv_q, ks_q, row_t)
    send_rows(1, row_t, home_t)

    loop(1, 16, lambda off: xz_recv(off).wait_recv())
    total = from_xz[0].astype(F32)
    for n in range(1, 16):
        total = total + from_xz[n].astype(F32)
    gathered[img] = total.astype(BF)

    def gather_send(off):
        peer = lax.rem(img + off, N_IMG)
        return pltpu.make_async_remote_copy(
            src_ref=gathered.at[img], dst_ref=gathered.at[img],
            send_sem=gsend.at[peer], recv_sem=grecv.at[img],
            device_id=(peer, me), device_id_type=MESH,
        )

    def gather_recv(off):
        peer = lax.rem(img + off, N_IMG)
        return pltpu.make_async_remote_copy(
            src_ref=gathered.at[peer], dst_ref=gathered.at[peer],
            send_sem=gsend.at[peer], recv_sem=grecv.at[peer],
            device_id=(peer, me), device_id_type=MESH,
        )

    loop(1, N_IMG, lambda off: gather_send(off).start())

    def receive_rows(kind, land):
        for e in range(2):
            here, copy = come_home_rows(kind, land, e)

            @pl.when(jnp.logical_not(here))
            def _():
                copy.wait_recv()

    peers(lambda peer: come_home(0, home_dq, peer).wait_recv())
    receive_rows(0, home_dq)
    peers(lambda peer: come_home(1, home_dk, peer).wait_recv())
    receive_sums(4, home_dkp)
    add_shared(home_dk, home_dkp)
    dquery = jnp.concatenate([unfold(home_dq, 0), unfold(home_dq, 1)], axis=0)
    dkey = jnp.concatenate([unfold(home_dk, 0), unfold(home_dk, 1)], axis=0)
    gradx[...] = (
        dot(dquery, wq[...], NT) + dot(dkey, wk[...], NT) + dot(dv2[core], wv[...], NT)
    ).astype(BF)
    gradx_copy = pltpu.make_async_copy(gradx, gradx_out.at[0], out_sem.at[0])
    gradx_copy.start()

    peers(lambda peer: come_home(2, home_t, peer).wait_recv())
    receive_rows(1, home_t)
    for r in range(2):
        mixed[r * ROWS // 2 : (r + 1) * ROWS // 2] = dot(unfold(home_t, r), wo[...]).astype(BF)
    mixed_copy = pltpu.make_async_copy(mixed, mixed_out.at[0], out_sem.at[1])
    mixed_copy.start()

    loop(1, N_IMG, lambda off: gather_recv(off).wait_recv())
    for kind in range(2):
        for n in range(4):
            final[kind, SLOT * n : SLOT * n + HALF] = gathered[4 * n + kind].astype(F32)
            final[kind, SLOT * n + HALF : SLOT * (n + 1)] = gathered[4 * n + 2 + kind][
                : SLOT - HALF
            ].astype(F32)
    for c in range(5):
        gv[:, 128 * c : 128 * c + 128] = final[0, 160 * c : 160 * c + 160]
    for c in range(10):
        go[:, 128 * c : 128 * c + 128] = final[1, 80 * c : 80 * c + 80]
    gv_copy = pltpu.make_async_copy(gv, gv_out, out_sem.at[2])
    go_copy = pltpu.make_async_copy(go, go_out, out_sem.at[3])
    gv_copy.start()
    go_copy.start()

    for kind, stage, land in ((0, st_kv, kv_w), (1, st_qd, qd_w), (2, st_ks, ks_w)):
        peers(lambda peer: to_whole(kind, stage, land, peer).wait_send())
    for kind, stage, land in ((0, st_kv, kv_q), (2, st_ks, ks_q)):
        def sent(e, n):
            peer, copy = to_quarter(kind, stage, land, e, n)

            @pl.when(peer != me)
            def _():
                copy.wait_send()

        each_quarter(sent)

    for e in range(2):
        here, copy = quarter_rows(e)

        @pl.when(jnp.logical_not(here))
        def _():
            copy.wait_send()

    @pl.when(holds)
    def _():
        hand_over(0, kv_q, kv_q).wait_send()
        hand_over(1, ks_q, ks_q).wait_send()
        peers(lambda peer: go_home(4, part_dk, home_dkp, peer).wait_send())
        peers(lambda peer: go_home(5, part_dv, home_dvp, peer).wait_send())

    @pl.when(jnp.logical_not(holds))
    def _():
        hand_over(2, part_dv, sib_dv).wait_send()
        hand_over(3, part_dk, sib_dk).wait_send()

    @pl.when(core == 1)
    def _():
        share(1, x2, 0).wait_send()
        dv_share.wait_send()

    @pl.when(core == 0)
    def _():
        share(0, g2, 1).wait_send()

    for kind, src, land in (
        (0, out_dq, home_dq), (1, out_dk, home_dk), (2, out_t, home_t),
        (3, out_dv, home_dv),
    ):
        peers(lambda peer: go_home(kind, src, land, peer).wait_send())
    for kind, src, land in ((0, row_dq, home_dq), (1, row_t, home_t)):
        for t in range(2):
            @pl.when(jnp.logical_not(owned(t)))
            def _():
                go_home_rows(kind, src, land, t).wait_send()

    for n in range(N_PATCH):
        @pl.when(jnp.logical_not(stays(n)))
        def _():
            a_home(n).wait_send()

    for t in range(2):
        @pl.when(jnp.logical_not(stays(first_q + t)))
        def _():
            a_home_rows(t).wait_send()

    for off in range(1, 4):
        y_copy(off).wait_send()
    loop(1, 16, lambda off: xz_send(off).wait_send())
    loop(1, N_IMG, lambda off: gather_send(off).wait_send())
    for copy in (gradx_copy, mixed_copy, gv_copy, go_copy):
        copy.wait()


def pass_on(*refs):
    sources, results, held = refs[:4], refs[4:8], refs[8:12]
    load_sem, store_sem = refs[12:]
    loads = [pltpu.make_async_copy(sources[n], held[n], load_sem.at[n]) for n in range(4)]
    stores = [pltpu.make_async_copy(held[n], results[n], store_sem.at[n]) for n in range(4)]
    for copy in loads:
        copy.start()
    for load, store in zip(loads, stores):
        load.wait()
        store.start()
    for store in stores:
        store.wait()


def vm(*shape, dtype=BF):
    return pltpu.VMEM(shape, dtype)


def dma(*shape):
    return pltpu.SemaphoreType.DMA(shape)


def on_device(latents_now, latents_stale, w_query, w_key, w_value, w_out, cotangent):
    half = ROWS // 2
    shapes = (
        jax.ShapeDtypeStruct((1, ROWS, C), BF),
        jax.ShapeDtypeStruct((1, ROWS, C), BF),
        jax.ShapeDtypeStruct((C // N_PATCH, INNER), F32),
        jax.ShapeDtypeStruct((INNER // N_PATCH, C), F32),
    )
    anywhere = pl.BlockSpec(memory_space=pl.ANY)
    results = pl.pallas_call(
        kernel,
        out_shape=shapes,
        in_specs=[anywhere] * 7,
        out_specs=[anywhere] * 4,
        scratch_shapes=[
            vm(2, ROWS, C), vm(2, ROWS, C), vm(ROWS, C), vm(C, INNER), vm(C, INNER), vm(C, INNER), vm(INNER, C),
            dma(7), dma(4),
            vm(10, ROWS, 128), vm(10, ROWS, 128), vm(10, ROWS, 128),
            vm(8, ROWS, 128), vm(8, ROWS, 128), vm(8, ROWS, 128),
            vm(8, ROWS, 128), vm(2, ROWS, 128), vm(8, ROWS, 128),
            dma(3, 8), dma(3, 8), dma(3, 8), dma(3, 8),
            vm(8, ROWS, TOKENS), vm(2, ROWS, TOKENS), vm(10, ROWS, 128, dtype=F32), vm(10, HEAD_DIM, ROWS),
            vm(HEAD_DIM, TOKENS, dtype=F32), vm(2, 8, ROWS, 128),
            vm(8, half, 128), vm(8, half, 128), vm(8, half, 128), vm(8, half, 128), vm(8, half, 128),
            vm(8, half, 128), vm(8, half, 128), vm(2, half, 128), vm(2, half, 128), vm(2, half, 128),
            vm(2, 10, half, 128), vm(10, half, 128), vm(10, half, 128), vm(10, half, 128), vm(10, half, 128),
            vm(8, half, 128), vm(8, half, 128), vm(8, half, 128), vm(8, half, 128), dma(4), dma(4),
            dma(6, 8), dma(6, 8), dma(2, 2), dma(2, 2), dma(8), dma(2, 8), dma(2), dma(2, 2),
            vm(C, 2 * ROWS), vm(2, ROWS, INNER), vm(8, PART, 128), vm(3, 8, SLOT, 128), vm(8, 2 * HALF, 128),
            vm(16, HALF, 128), vm(16, HALF, 128), vm(2, PART, 128, dtype=F32),
            vm(ROWS, C), vm(ROWS, C), vm(C // N_PATCH, INNER, dtype=F32), vm(INNER // N_PATCH, C, dtype=F32),
            dma(2), dma(3), dma(3), dma(16), dma(16), dma(16), dma(16), dma(4),
        ],
        compiler_params=pltpu.CompilerParams(
            collective_id=0, has_side_effects=True, vmem_limit_bytes=56 * 2**20
        ),
        cost_estimate=pl.CostEstimate(flops=10**10, bytes_accessed=12 * 2**20, transcendentals=10**7),
    )(latents_now[0], latents_stale[0], w_query, w_key, w_value, w_out, cotangent[0])
    return pl.pallas_call(
        pass_on,
        out_shape=shapes,
        in_specs=[anywhere] * 4,
        out_specs=[anywhere] * 4,
        scratch_shapes=[pltpu.VMEM(shape.shape, shape.dtype) for shape in shapes] + [dma(4), dma(4)],
        compiler_params=pltpu.CompilerParams(vmem_limit_bytes=56 * 2**20),
        cost_estimate=pl.CostEstimate(flops=0, bytes_accessed=2 * 2**20, transcendentals=0),
    )(*results)


def solution(mesh):
    rows = P("img", "patch", None)
    return jax.shard_map(
        on_device,
        mesh=mesh,
        in_specs=(rows, rows, P(), P(), P(), P(), rows),
        out_specs=(rows, rows, P("patch", None), P("patch", None)),
        check_vma=False,
    )
```

```python
import jax
import jax.numpy as jnp
from jax import lax
from jax.experimental import pallas as pl
from jax.experimental.pallas import tpu as pltpu
from jax.sharding import PartitionSpec as P

HEADS = 10
HEAD_DIM = 64
N_PATCH = 8
N_IMG = 16
ROWS = 256
TOKENS = 2048
C = 1280
INNER = 640
PART = 832
SLOT = 208
HALF = 112
BF = jnp.bfloat16
F32 = jnp.float32
MESH = pl.DeviceIdType.MESH
NT = (((1,), (1,)), ((), ()))
NN = (((1,), (0,)), ((), ()))
SCALE = HEAD_DIM**-0.5
EXP2_SCALE = SCALE * 1.4426950408889634


def dot(a, b, dims=NN):
    return lax.dot_general(a, b, dims, preferred_element_type=F32)


def left_half(rows):
    return lax.broadcasted_iota(jnp.int32, (rows, 128), 1) < HEAD_DIM


def pair(a, b):
    return jnp.concatenate([a, b], axis=1)


def fold(x, lo):
    cols = slice(lo, lo + HEAD_DIM)
    return pair(x[: ROWS // 2, cols], x[ROWS // 2 :, cols])


def probabilities(qd, kv):
    left = left_half(ROWS)
    scores = dot(jnp.where(left, qd, jnp.zeros_like(qd)), kv, NT)
    top = jnp.max(scores, axis=1, keepdims=True)
    e = jnp.exp2((scores - top) * EXP2_SCALE)
    inv = 1.0 / jnp.sum(e, axis=1, keepdims=True)
    return e.astype(BF), inv


def both(parts, axis):
    return jnp.concatenate(parts, axis=axis)


def fresh_first(blocks, kv, acc):
    left = left_half(ROWS)
    outs, terms, rows = [], [], []
    for qd in blocks:
        e16, inv = probabilities(qd, kv)
        a16 = (dot(e16, kv) * inv).astype(BF)
        delta = jnp.sum(
            jnp.where(left, 0.0, a16.astype(F32) * qd.astype(F32)), axis=1, keepdims=True
        )
        scaled = (qd.astype(F32) * jnp.where(left, inv * SCALE, inv)).T.astype(BF)
        outs.append((e16, fold(a16, HEAD_DIM), jnp.where(left, inv * SCALE, delta), scaled[:HEAD_DIM]))
        terms.append(e16)
        rows.append(scaled[HEAD_DIM:])
    acc[...] += dot(both(rows, 1), both(terms, 0))
    return outs


def fresh_second(blocks, kv, es, stats, q_scaled, acc):
    left = left_half(ROWS)
    outs, terms = [], []
    for qd, e16, row in zip(blocks, es, stats):
        dprob = dot(jnp.where(left, jnp.zeros_like(qd), qd), kv, NT)
        ds = (e16.astype(F32) * (dprob - row[:, HEAD_DIM : HEAD_DIM + 1])).astype(BF)
        outs.append(fold((dot(ds, kv) * row[:, 0:1]).astype(BF), 0))
        terms.append(ds)
    acc[...] += dot(both(q_scaled, 1), both(terms, 0))
    return outs


def stale_tile(qd, kv):
    e16, inv = probabilities(qd, kv)
    return fold((dot(e16, kv) * inv).astype(BF), HEAD_DIM)


def loop(lo, hi, fn):
    def step(n, carry):
        fn(n)
        return carry

    lax.fori_loop(lo, hi, step, 0)


def kernel(
    x_hbm, s_hbm, wq_hbm, wk_hbm, wv_hbm, wo_hbm, g_hbm,
    mixed_out, gradx_out, gv_out, go_out,
    x2, g2, s, wq, wk, wv, wo, load_sem, share_sem,
    st_kv, st_qd, st_ks,
    kv_w, qd_w, ks_w, kv_q, qd_q, ks_q,
    send_w, recv_w, send_q, recv_q,
    e_w, e_q, stats, q_scaled, acc, kmix,
    out_a, out_dq, out_t, out_dv, out_dk, part_dv, part_dk, row_a, row_dq, row_t,
    home_a, home_dq, home_t, home_dv, home_dk, home_dvp, home_dkp, sib_dv, sib_dk, pair_send, pair_recv,
    hsend, hrecv, psend, precv, asend, arecv, apsend, aprecv,
    x_t, dv2, grads, from_y, ysum, from_xz, gathered, final,
    mixed, gradx, gv, go,
    dsem, ysend, yrecv, xsend, xrecv, gsend, grecv, out_sem,
):
    img = lax.axis_index("img")
    me = lax.axis_index("patch")
    core = lax.rem(img, 2)
    zlo = lax.rem(img // 2, 2)
    yy = img // 4
    mine_e = me // 4
    shared_core = lax.rem(me // 2, 2)
    shared_img = img - core + shared_core
    holds = core == shared_core
    first_q = 4 * lax.rem(me, 2) + 2 * core
    my_helper_core = lax.rem(me, 4) // 2

    def helper(c, e):
        return img - core + my_helper_core, 4 * e + 2 * c + me // 4
    core_one = img - core + 1
    sibling = img + 1 - 2 * core

    loads = [
        pltpu.make_async_copy(src, dst, load_sem.at[n])
        for n, (src, dst) in enumerate(
            (
                (x_hbm, x2.at[core]), (wk_hbm, wk), (wv_hbm, wv), (wq_hbm, wq),
                (g_hbm, g2.at[core]), (wo_hbm, wo), (s_hbm, s),
            )
        )
    ]
    for copy in loads[:3]:
        copy.start()

    barrier = pltpu.get_barrier_semaphore()
    for off in range(1, N_PATCH):
        pl.semaphore_signal(
            barrier, inc=1, device_id=(img, lax.rem(me + off, N_PATCH)), device_id_type=MESH
        )
    for off in range(1, N_IMG):
        pl.semaphore_signal(
            barrier, inc=1, device_id=(lax.rem(img + off, N_IMG), me), device_id_type=MESH
        )
    for off in range(1, N_PATCH):
        for there in (img + 2 - 4 * zlo, sibling):
            pl.semaphore_signal(
                barrier, inc=1, device_id=(there, lax.rem(me + off, N_PATCH)), device_id_type=MESH
            )

    def turn(off, sign=1):
        dx = off % 4 if sign == 1 else 4 - off % 4
        return lax.rem(me // 4 + off // 4, 2) * 4 + lax.rem(me + dx, 4)

    def peers(fn):
        for off in (5, 1, 7, 3, 4, 6, 2):
            fn(turn(off))

    def to_whole(kind, stage, land, peer):
        return pltpu.make_async_remote_copy(
            src_ref=stage.at[peer], dst_ref=land.at[me],
            send_sem=send_w.at[kind, peer], recv_sem=recv_w.at[kind, me],
            device_id=(img, peer), device_id_type=MESH,
        )

    def from_whole(kind, land, peer):
        return pltpu.make_async_remote_copy(
            src_ref=land.at[peer], dst_ref=land.at[peer],
            send_sem=send_w.at[kind, peer], recv_sem=recv_w.at[kind, peer],
            device_id=(img, peer), device_id_type=MESH,
        )

    def to_quarter(kind, stage, land, e, n):
        peer = 4 * e + 2 * core + n
        return peer, pltpu.make_async_remote_copy(
            src_ref=stage.at[N_PATCH + e], dst_ref=land.at[me],
            send_sem=send_q.at[kind, peer], recv_sem=recv_q.at[kind, me],
            device_id=(img, peer), device_id_type=MESH,
        )

    def each_quarter(fn):
        for e in range(2):
            for n in range(2):
                fn(e, n)

    def send_quarter(kind, stage, land):
        def one(e, n):
            peer, copy = to_quarter(kind, stage, land, e, n)

            @pl.when(peer != me)
            def _():
                copy.start()

        each_quarter(one)

        @pl.when(holds)
        def _():
            land[me] = stage[N_PATCH + mine_e]

    def from_quarter(kind, land, peer):
        return pltpu.make_async_remote_copy(
            src_ref=land.at[peer], dst_ref=land.at[peer],
            send_sem=send_q.at[kind, peer], recv_sem=recv_q.at[kind, peer],
            device_id=(img, peer), device_id_type=MESH,
        )

    def hand_over(n, src, dst):
        return pltpu.make_async_remote_copy(
            src_ref=src, dst_ref=dst, send_sem=pair_send.at[n], recv_sem=pair_recv.at[n],
            device_id=(sibling, me), device_id_type=MESH,
        )

    def pass_keys(n, kind, land):
        @pl.when(holds)
        def _():
            peers(lambda peer: from_quarter(kind, land, peer).wait_recv())
            hand_over(n, land, land).start()

    def wait_keys(n, land):
        @pl.when(jnp.logical_not(holds))
        def _():
            hand_over(n, land, land).wait_recv()

    def pass_sums(n, part, arrived):
        @pl.when(jnp.logical_not(holds))
        def _():
            hand_over(n, part, arrived).start()

    def send_sums(n, kind, part, arrived, land):
        @pl.when(holds)
        def _():
            hand_over(n, part, arrived).wait_recv()
            part[...] = (part[...].astype(F32) + arrived[...].astype(F32)).astype(BF)
            peers(lambda peer: go_home(kind, part, land, peer).start())
            land[me] = part[me]

    def receive_sums(kind, land):
        def one(e, n):
            peer = 4 * e + 2 * core + n

            @pl.when(peer != me)
            def _():
                come_home(kind, land, peer).wait_recv()

        each_quarter(one)

    def quarter_rows(e):
        there, peer = helper(core, e)
        here = jnp.logical_and(there == img, peer == me)
        return here, pltpu.make_async_remote_copy(
            src_ref=st_qd.at[N_PATCH + e], dst_ref=qd_q.at[lax.rem(me, 2)],
            send_sem=send_q.at[1, e], recv_sem=recv_q.at[1, lax.rem(me, 2)],
            device_id=(there, peer), device_id_type=MESH,
        )

    def owned(t):
        return jnp.logical_and(holds, first_q + t == me)

    def quarter_rows_in(t):
        return pltpu.make_async_remote_copy(
            src_ref=qd_q.at[t], dst_ref=qd_q.at[t],
            send_sem=send_q.at[1, t], recv_sem=recv_q.at[1, t],
            device_id=(shared_img, first_q + t), device_id_type=MESH,
        )

    def share(core_from, ref, n):
        return pltpu.make_async_remote_copy(
            src_ref=ref.at[core_from], dst_ref=ref.at[core_from],
            send_sem=share_sem.at[n], recv_sem=share_sem.at[2 + n],
            device_id=(sibling, me), device_id_type=MESH,
        )

    def stage_pairs(stage, a, b):
        for h in range(HEADS):
            cols = slice(h * HEAD_DIM, (h + 1) * HEAD_DIM)
            stage[h] = pair(a[:, cols], b[:, cols])

    loads[0].wait()
    loads[1].wait()
    for copy in loads[3:]:
        copy.start()
    key = dot(x2[core], wk[...]).astype(BF)
    loads[2].wait()
    value = dot(x2[core], wv[...]).astype(BF)
    stage_pairs(st_kv, key, value)
    pl.semaphore_wait(barrier, 3 * (N_PATCH - 1) + N_IMG - 1)
    peers(lambda peer: to_whole(0, st_kv, kv_w, peer).start())
    kv_w[me] = st_kv[me]
    loads[3].wait()
    query = dot(x2[core], wq[...]).astype(BF)
    loads[4].wait()
    loads[5].wait()
    dattend = dot(g2[core], wo[...], NT).astype(BF)
    stage_pairs(st_qd, query, dattend)
    for off in range(1, N_PATCH):
        to_whole(1, st_qd, qd_w, turn(off, -1)).start()
    qd_w[me] = st_qd[me]
    send_quarter(0, st_kv, kv_q)
    for e in range(2):
        here, copy = quarter_rows(e)

        @pl.when(jnp.logical_not(here))
        def _():
            copy.start()

        @pl.when(here)
        def _():
            qd_q[lax.rem(me, 2)] = st_qd[N_PATCH + e]

    @pl.when(core == 1)
    def _():
        share(1, x2, 0).start()

    @pl.when(core == 0)
    def _():
        share(0, g2, 1).start()

    loads[6].wait()
    key_old = dot(s[...], wk[...]).astype(BF)
    value_old = dot(s[...], wv[...]).astype(BF)
    stage_pairs(st_ks, key_old, value_old)
    ks_w[me] = st_ks[me]

    @pl.when(core == 0)
    def _():
        share(1, x2, 0).wait_recv()
        x_t[:, :ROWS] = x2[0].T
        x_t[:, ROWS:] = x2[1].T

    @pl.when(core == 1)
    def _():
        share(0, g2, 1).wait_recv()

    def go_home(kind, src, land, peer):
        return pltpu.make_async_remote_copy(
            src_ref=src.at[peer], dst_ref=land.at[me],
            send_sem=hsend.at[kind, peer], recv_sem=hrecv.at[kind, me],
            device_id=(img, peer), device_id_type=MESH,
        )

    def come_home(kind, land, peer):
        return pltpu.make_async_remote_copy(
            src_ref=land.at[peer], dst_ref=land.at[peer],
            send_sem=hsend.at[kind, peer], recv_sem=hrecv.at[kind, peer],
            device_id=(img, peer), device_id_type=MESH,
        )

    def go_home_rows(kind, src, land, t):
        return pltpu.make_async_remote_copy(
            src_ref=src.at[t], dst_ref=land.at[N_PATCH + mine_e],
            send_sem=psend.at[kind, t], recv_sem=precv.at[kind, mine_e],
            device_id=(shared_img, first_q + t), device_id_type=MESH,
        )

    def come_home_rows(kind, land, e):
        there, peer = helper(core, e)
        here = jnp.logical_and(there == img, peer == me)
        return here, pltpu.make_async_remote_copy(
            src_ref=land.at[N_PATCH + e], dst_ref=land.at[N_PATCH + e],
            send_sem=psend.at[kind, e], recv_sem=precv.at[kind, e],
            device_id=(there, peer), device_id_type=MESH,
        )

    def a_home(i):
        return pltpu.make_async_remote_copy(
            src_ref=out_a.at[i], dst_ref=home_a.at[core, me],
            send_sem=asend.at[i], recv_sem=arecv.at[core, me],
            device_id=(core_one, i), device_id_type=MESH,
        )

    def a_in(c, peer):
        return pltpu.make_async_remote_copy(
            src_ref=home_a.at[c, peer], dst_ref=home_a.at[c, peer],
            send_sem=asend.at[peer], recv_sem=arecv.at[c, peer],
            device_id=(core_one, peer), device_id_type=MESH,
        )

    def a_home_rows(t):
        return pltpu.make_async_remote_copy(
            src_ref=row_a.at[t], dst_ref=home_a.at[shared_core, N_PATCH + mine_e],
            send_sem=apsend.at[t], recv_sem=aprecv.at[shared_core, mine_e],
            device_id=(core_one, first_q + t), device_id_type=MESH,
        )

    def a_in_rows(c, e):
        return pltpu.make_async_remote_copy(
            src_ref=home_a.at[c, N_PATCH + e], dst_ref=home_a.at[c, N_PATCH + e],
            send_sem=apsend.at[e], recv_sem=aprecv.at[c, e],
            device_id=helper(c, e), device_id_type=MESH,
        )

    def stays(peer):
        return jnp.logical_and(peer == me, core == 1)

    def put(out):
        for j in range(N_PATCH):
            out[j] = fold(acc[:, j * ROWS : (j + 1) * ROWS].T.astype(BF), 0)

    def clear():
        acc[...] = jnp.zeros_like(acc)

    peers(lambda peer: from_whole(0, kv_w, peer).wait_recv())
    clear()

    def first_pair(i, qd, kv, e, a):
        outs = fresh_first([qd[n] for n in i[0]], kv[...].reshape(TOKENS, 128), acc)
        for n, at, out in zip(*i, outs):
            e[n], a[n], stats[at], q_scaled[at] = out

    def two(k):
        return turn(2 * k), turn(2 * k + 1)

    def first_whole(k):
        i = two(k)

        @pl.when(k == 3)
        def _():
            pass_keys(0, 0, kv_q)

        for n in i:
            @pl.when(n != me)
            def _():
                from_whole(1, qd_w, n).wait_recv()

        first_pair((i, i), qd_w, kv_w, e_w, out_a)
        for n in i:
            @pl.when(jnp.logical_not(stays(n)))
            def _():
                a_home(n).start()

    loop(0, 4, first_whole)

    @pl.when(core == 1)
    def _():
        home_a[1, me] = out_a[me]

    put(out_dv)
    peers(lambda peer: go_home(3, out_dv, home_dv, peer).start())
    home_dv[me] = out_dv[me]

    wait_keys(0, kv_q)
    for t in range(2):
        @pl.when(jnp.logical_not(owned(t)))
        def _():
            quarter_rows_in(t).wait_recv()

    clear()

    first_pair(((0, 1), (N_PATCH, N_PATCH + 1)), qd_q, kv_q, e_q, row_a)
    for t in range(2):
        here = stays(first_q + t)

        @pl.when(jnp.logical_not(here))
        def _():
            a_home_rows(t).start()

        @pl.when(here)
        def _():
            home_a[shared_core, N_PATCH + mine_e] = row_a[t]

    put(part_dv)
    pass_sums(2, part_dv, sib_dv)
    send_sums(2, 5, part_dv, sib_dv, home_dvp)
    peers(lambda peer: to_whole(2, st_ks, ks_w, peer).start())
    send_quarter(2, st_ks, ks_q)

    def unfold(src, r):
        cols = slice(r * HEAD_DIM, (r + 1) * HEAD_DIM)
        return jnp.concatenate([src[h][:, cols] for h in range(HEADS)], axis=1)

    def add_shared(land, parts):
        for e in range(2):
            first = 4 * e + 2 * core
            total = parts[first].astype(F32) + parts[first + 1].astype(F32)
            land[N_PATCH + e] = total.astype(BF)

    def y_copy(off):
        peer = lax.rem(yy + off, 4)
        return pltpu.make_async_remote_copy(
            src_ref=grads.at[:, pl.ds(pl.multiple_of(SLOT * peer, 16), SLOT)],
            dst_ref=from_y.at[off - 1],
            send_sem=ysend.at[off - 1], recv_sem=yrecv.at[off - 1],
            device_id=(4 * peer + 2 * zlo + core, me), device_id_type=MESH,
        )

    grads[:, 800:] = jnp.zeros((N_PATCH, PART - 800, 128), BF)

    def make_grad_out():
        @pl.when(core == 1)
        def _():
            for c in range(2):
                for n in range(N_PATCH):
                    if c == 1:
                        @pl.when(n != me)
                        def _():
                            a_in(c, n).wait_recv()
                    else:
                        a_in(c, n).wait_recv()
                for e in range(2):
                    there, peer = helper(c, e)

                    @pl.when(jnp.logical_not(jnp.logical_and(there == img, peer == me)))
                    def _():
                        a_in_rows(c, e).wait_recv()
            a_t = jnp.concatenate(
                [unfold(home_a.at[c], r).T for c in range(2) for r in range(2)], axis=1
            )
            g_all = g2[...].reshape(2 * ROWS, C)
            for q in range(N_PATCH):
                part = dot(a_t[80 * q : 80 * q + 80], g_all).astype(BF)
                for c in range(10):
                    grads[q, 80 * c : 80 * c + 80] = part[:, 128 * c : 128 * c + 128]
            for off in range(1, 4):
                y_copy(off).start()

    dv_share = pltpu.make_async_remote_copy(
        src_ref=dv2.at[1], dst_ref=dv2.at[1], send_sem=dsem.at[0], recv_sem=dsem.at[1],
        device_id=(sibling, me), device_id_type=MESH,
    )

    def make_grad_value():

        peers(lambda peer: come_home(3, home_dv, peer).wait_recv())
        receive_sums(5, home_dvp)
        add_shared(home_dv, home_dvp)
        for r in range(2):
            dv2[core, r * ROWS // 2 : (r + 1) * ROWS // 2] = unfold(home_dv, r)
        @pl.when(core == 1)
        def _():
            dv_share.start()

        @pl.when(core == 0)
        def _():
            dv_share.wait_recv()
            dv_all = dv2[...].reshape(2 * ROWS, INNER)
            for q in range(N_PATCH):
                part = dot(x_t[160 * q : 160 * q + 160], dv_all).astype(BF)
                for c in range(5):
                    grads[q, 160 * c : 160 * c + 160] = part[:, 128 * c : 128 * c + 128]
            for off in range(1, 4):
                y_copy(off).start()

    clear()

    def second_pair(i, qd, kv, e, out):
        dqs = fresh_second(
            [qd[n] for n in i[0]], kv[...].reshape(TOKENS, 128), [e[n] for n in i[0]],
            [stats[n] for n in i[1]], [q_scaled[n] for n in i[1]], acc,
        )
        for n, dq in zip(i[0], dqs):
            out[n] = dq

    def second_whole(k):
        i = two(k)

        @pl.when(k == 1)
        def _():
            make_grad_out()

        @pl.when(k == 2)
        def _():
            make_grad_value()

        second_pair((i, i), qd_w, kv_w, e_w, out_dq)
        for n in i:
            @pl.when(n != me)
            def _():
                go_home(0, out_dq, home_dq, n).start()

    loop(0, 4, second_whole)
    home_dq[me] = out_dq[me]
    put(out_dk)
    peers(lambda peer: go_home(1, out_dk, home_dk, peer).start())
    home_dk[me] = out_dk[me]

    clear()

    second_pair(((0, 1), (N_PATCH, N_PATCH + 1)), qd_q, kv_q, e_q, row_dq)

    def send_rows(kind, src, land):
        for t in range(2):
            @pl.when(jnp.logical_not(owned(t)))
            def _():
                go_home_rows(kind, src, land, t).start()

            @pl.when(owned(t))
            def _():
                land[N_PATCH + mine_e] = src[t]

    send_rows(0, row_dq, home_dq)
    put(part_dk)
    pass_sums(3, part_dk, sib_dk)

    plane = zlo * N_PATCH + me

    def xz_peer(off):
        there = lax.rem(plane + off, 16)
        return there, there // N_PATCH, lax.rem(there, N_PATCH)

    def xz_send(off):
        there, z_there, p_there = xz_peer(off)
        return pltpu.make_async_remote_copy(
            src_ref=ysum.at[p_there, pl.ds(pl.multiple_of(HALF * z_there, 16), HALF)],
            dst_ref=from_xz.at[plane],
            send_sem=xsend.at[there], recv_sem=xrecv.at[plane],
            device_id=(4 * yy + 2 * z_there + core, p_there), device_id_type=MESH,
        )

    def xz_recv(off):
        there, z_there, p_there = xz_peer(off)
        return pltpu.make_async_remote_copy(
            src_ref=from_xz.at[there], dst_ref=from_xz.at[there],
            send_sem=xsend.at[there], recv_sem=xrecv.at[there],
            device_id=(4 * yy + 2 * z_there + core, p_there), device_id_type=MESH,
        )

    def sum_over_y():
        for off in range(1, 4):
            y_copy(off).wait_recv()

        def y_add(q):
            total = grads[q, pl.ds(pl.multiple_of(SLOT * yy, 16), SLOT)].astype(F32)
            for n in range(3):
                total = total + from_y[n, q].astype(F32)
            ysum[q, :SLOT] = total.astype(BF)
            ysum[q, SLOT:] = jnp.zeros((2 * HALF - SLOT, 128), BF)

        loop(0, N_PATCH, y_add)
        loop(1, 16, lambda off: xz_send(off).start())
        from_xz[plane] = ysum[me, pl.ds(pl.multiple_of(HALF * zlo, 16), HALF)]

    peers(lambda peer: from_whole(2, ks_w, peer).wait_recv())
    kmix[0] = ks_w[...]
    kmix[1] = ks_w[...]

    def stale_pair(at, i, qd, kv, ks, out):
        for t in range(2):
            kmix[t, i[t]] = kv[i[t]]
        outs = [stale_tile(qd[at[t]], kmix[t].reshape(TOKENS, 128)) for t in range(2)]
        for t in range(2):
            out[at[t]] = outs[t]
            kmix[t, i[t]] = ks[i[t]]

    def stale_whole(k):
        i = two(k)

        @pl.when(k == 4)
        def _():
            sum_over_y()

        @pl.when(k == 1)
        def _():
            send_sums(3, 4, part_dk, sib_dk, home_dkp)

        @pl.when(k == 3)
        def _():
            pass_keys(1, 2, ks_q)

        stale_pair(i, i, qd_w, kv_w, ks_w, out_t)
        for n in i:
            @pl.when(n != me)
            def _():
                go_home(2, out_t, home_t, n).start()

    loop(0, 4, stale_whole)
    home_t[me] = out_t[me]
    sum_over_y()
    wait_keys(1, ks_q)
    kmix[0] = ks_q[...]
    kmix[1] = ks_q[...]

    stale_pair((0, 1), (first_q, first_q + 1), qd_q, kv_q, ks_q, row_t)
    send_rows(1, row_t, home_t)

    loop(1, 16, lambda off: xz_recv(off).wait_recv())
    total = from_xz[0].astype(F32)
    for n in range(1, 16):
        total = total + from_xz[n].astype(F32)
    gathered[img] = total.astype(BF)

    def gather_send(off):
        peer = lax.rem(img + off, N_IMG)
        return pltpu.make_async_remote_copy(
            src_ref=gathered.at[img], dst_ref=gathered.at[img],
            send_sem=gsend.at[peer], recv_sem=grecv.at[img],
            device_id=(peer, me), device_id_type=MESH,
        )

    def gather_recv(off):
        peer = lax.rem(img + off, N_IMG)
        return pltpu.make_async_remote_copy(
            src_ref=gathered.at[peer], dst_ref=gathered.at[peer],
            send_sem=gsend.at[peer], recv_sem=grecv.at[peer],
            device_id=(peer, me), device_id_type=MESH,
        )

    loop(1, N_IMG, lambda off: gather_send(off).start())

    def receive_rows(kind, land):
        for e in range(2):
            here, copy = come_home_rows(kind, land, e)

            @pl.when(jnp.logical_not(here))
            def _():
                copy.wait_recv()

    peers(lambda peer: come_home(0, home_dq, peer).wait_recv())
    receive_rows(0, home_dq)
    peers(lambda peer: come_home(1, home_dk, peer).wait_recv())
    receive_sums(4, home_dkp)
    add_shared(home_dk, home_dkp)
    dquery = jnp.concatenate([unfold(home_dq, 0), unfold(home_dq, 1)], axis=0)
    dkey = jnp.concatenate([unfold(home_dk, 0), unfold(home_dk, 1)], axis=0)
    gradx[...] = (
        dot(dquery, wq[...], NT) + dot(dkey, wk[...], NT) + dot(dv2[core], wv[...], NT)
    ).astype(BF)
    gradx_copy = pltpu.make_async_copy(gradx, gradx_out.at[0], out_sem.at[0])
    gradx_copy.start()

    peers(lambda peer: come_home(2, home_t, peer).wait_recv())
    receive_rows(1, home_t)
    for r in range(2):
        mixed[r * ROWS // 2 : (r + 1) * ROWS // 2] = dot(unfold(home_t, r), wo[...]).astype(BF)
    mixed_copy = pltpu.make_async_copy(mixed, mixed_out.at[0], out_sem.at[1])
    mixed_copy.start()

    loop(1, N_IMG, lambda off: gather_recv(off).wait_recv())
    for kind in range(2):
        for n in range(4):
            final[kind, SLOT * n : SLOT * n + HALF] = gathered[4 * n + kind].astype(F32)
            final[kind, SLOT * n + HALF : SLOT * (n + 1)] = gathered[4 * n + 2 + kind][
                : SLOT - HALF
            ].astype(F32)
    for c in range(5):
        gv[:, 128 * c : 128 * c + 128] = final[0, 160 * c : 160 * c + 160]
    for c in range(10):
        go[:, 128 * c : 128 * c + 128] = final[1, 80 * c : 80 * c + 80]
    gv_copy = pltpu.make_async_copy(gv, gv_out, out_sem.at[2])
    go_copy = pltpu.make_async_copy(go, go_out, out_sem.at[3])
    gv_copy.start()
    go_copy.start()

    for kind, stage, land in ((0, st_kv, kv_w), (1, st_qd, qd_w), (2, st_ks, ks_w)):
        peers(lambda peer: to_whole(kind, stage, land, peer).wait_send())
    for kind, stage, land in ((0, st_kv, kv_q), (2, st_ks, ks_q)):
        def sent(e, n):
            peer, copy = to_quarter(kind, stage, land, e, n)

            @pl.when(peer != me)
            def _():
                copy.wait_send()

        each_quarter(sent)

    for e in range(2):
        here, copy = quarter_rows(e)

        @pl.when(jnp.logical_not(here))
        def _():
            copy.wait_send()

    @pl.when(holds)
    def _():
        hand_over(0, kv_q, kv_q).wait_send()
        hand_over(1, ks_q, ks_q).wait_send()
        peers(lambda peer: go_home(4, part_dk, home_dkp, peer).wait_send())
        peers(lambda peer: go_home(5, part_dv, home_dvp, peer).wait_send())

    @pl.when(jnp.logical_not(holds))
    def _():
        hand_over(2, part_dv, sib_dv).wait_send()
        hand_over(3, part_dk, sib_dk).wait_send()

    @pl.when(core == 1)
    def _():
        share(1, x2, 0).wait_send()
        dv_share.wait_send()

    @pl.when(core == 0)
    def _():
        share(0, g2, 1).wait_send()

    for kind, src, land in (
        (0, out_dq, home_dq), (1, out_dk, home_dk), (2, out_t, home_t),
        (3, out_dv, home_dv),
    ):
        peers(lambda peer: go_home(kind, src, land, peer).wait_send())
    for kind, src, land in ((0, row_dq, home_dq), (1, row_t, home_t)):
        for t in range(2):
            @pl.when(jnp.logical_not(owned(t)))
            def _():
                go_home_rows(kind, src, land, t).wait_send()

    for n in range(N_PATCH):
        @pl.when(jnp.logical_not(stays(n)))
        def _():
            a_home(n).wait_send()

    for t in range(2):
        @pl.when(jnp.logical_not(stays(first_q + t)))
        def _():
            a_home_rows(t).wait_send()

    for off in range(1, 4):
        y_copy(off).wait_send()
    loop(1, 16, lambda off: xz_send(off).wait_send())
    loop(1, N_IMG, lambda off: gather_send(off).wait_send())
    for copy in (gradx_copy, mixed_copy, gv_copy, go_copy):
        copy.wait()


def pass_on(*refs):
    sources, results, held = refs[:4], refs[4:8], refs[8:12]
    load_sem, store_sem = refs[12:]
    loads = [pltpu.make_async_copy(sources[n], held[n], load_sem.at[n]) for n in range(4)]
    stores = [pltpu.make_async_copy(held[n], results[n], store_sem.at[n]) for n in range(4)]
    for copy in loads:
        copy.start()
    for load, store in zip(loads, stores):
        load.wait()
        store.start()
    for store in stores:
        store.wait()


def vm(*shape, dtype=BF):
    return pltpu.VMEM(shape, dtype)


def dma(*shape):
    return pltpu.SemaphoreType.DMA(shape)


def on_device(latents_now, latents_stale, w_query, w_key, w_value, w_out, cotangent):
    half = ROWS // 2
    shapes = (
        jax.ShapeDtypeStruct((1, ROWS, C), BF),
        jax.ShapeDtypeStruct((1, ROWS, C), BF),
        jax.ShapeDtypeStruct((C // N_PATCH, INNER), F32),
        jax.ShapeDtypeStruct((INNER // N_PATCH, C), F32),
    )
    anywhere = pl.BlockSpec(memory_space=pl.ANY)
    results = pl.pallas_call(
        kernel,
        out_shape=shapes,
        in_specs=[anywhere] * 7,
        out_specs=[anywhere] * 4,
        scratch_shapes=[
            vm(2, ROWS, C), vm(2, ROWS, C), vm(ROWS, C), vm(C, INNER), vm(C, INNER), vm(C, INNER), vm(INNER, C),
            dma(7), dma(4),
            vm(10, ROWS, 128), vm(10, ROWS, 128), vm(10, ROWS, 128),
            vm(8, ROWS, 128), vm(8, ROWS, 128), vm(8, ROWS, 128),
            vm(8, ROWS, 128), vm(2, ROWS, 128), vm(8, ROWS, 128),
            dma(3, 8), dma(3, 8), dma(3, 8), dma(3, 8),
            vm(8, ROWS, TOKENS), vm(2, ROWS, TOKENS), vm(10, ROWS, 128, dtype=F32), vm(10, HEAD_DIM, ROWS),
            vm(HEAD_DIM, TOKENS, dtype=F32), vm(2, 8, ROWS, 128),
            vm(8, half, 128), vm(8, half, 128), vm(8, half, 128), vm(8, half, 128), vm(8, half, 128),
            vm(8, half, 128), vm(8, half, 128), vm(2, half, 128), vm(2, half, 128), vm(2, half, 128),
            vm(2, 10, half, 128), vm(10, half, 128), vm(10, half, 128), vm(10, half, 128), vm(10, half, 128),
            vm(8, half, 128), vm(8, half, 128), vm(8, half, 128), vm(8, half, 128), dma(4), dma(4),
            dma(6, 8), dma(6, 8), dma(2, 2), dma(2, 2), dma(8), dma(2, 8), dma(2), dma(2, 2),
            vm(C, 2 * ROWS), vm(2, ROWS, INNER), vm(8, PART, 128), vm(3, 8, SLOT, 128), vm(8, 2 * HALF, 128),
            vm(16, HALF, 128), vm(16, HALF, 128), vm(2, PART, 128, dtype=F32),
            vm(ROWS, C), vm(ROWS, C), vm(C // N_PATCH, INNER, dtype=F32), vm(INNER // N_PATCH, C, dtype=F32),
            dma(2), dma(3), dma(3), dma(16), dma(16), dma(16), dma(16), dma(4),
        ],
        compiler_params=pltpu.CompilerParams(
            collective_id=0, has_side_effects=True, vmem_limit_bytes=56 * 2**20
        ),
        cost_estimate=pl.CostEstimate(flops=10**10, bytes_accessed=12 * 2**20, transcendentals=10**7),
    )(latents_now[0], latents_stale[0], w_query, w_key, w_value, w_out, cotangent[0])
    return pl.pallas_call(
        pass_on,
        out_shape=shapes,
        in_specs=[anywhere] * 4,
        out_specs=[anywhere] * 4,
        scratch_shapes=[pltpu.VMEM(shape.shape, shape.dtype) for shape in shapes] + [dma(4), dma(4)],
        compiler_params=pltpu.CompilerParams(vmem_limit_bytes=56 * 2**20),
        cost_estimate=pl.CostEstimate(flops=0, bytes_accessed=2 * 2**20, transcendentals=0),
    )(*results)


def solution(mesh):
    rows = P("img", "patch", None)
    return jax.shard_map(
        on_device,
        mesh=mesh,
        in_specs=(rows, rows, P(), P(), P(), P(), rows),
        out_specs=(rows, rows, P("patch", None), P("patch", None)),
        check_vma=False,
    )
```

```python
import jax
import jax.numpy as jnp
from jax import lax
from jax.experimental import pallas as pl
from jax.experimental.pallas import tpu as pltpu
from jax.sharding import PartitionSpec as P

HEADS = 10
HEAD_DIM = 64
N_PATCH = 8
N_IMG = 16
ROWS = 256
TOKENS = 2048
C = 1280
INNER = 640
PART = 832
SLOT = 208
HALF = 112
BF = jnp.bfloat16
F32 = jnp.float32
MESH = pl.DeviceIdType.MESH
NT = (((1,), (1,)), ((), ()))
NN = (((1,), (0,)), ((), ()))
SCALE = HEAD_DIM**-0.5
EXP2_SCALE = SCALE * 1.4426950408889634


def dot(a, b, dims=NN):
    return lax.dot_general(a, b, dims, preferred_element_type=F32)


def left_half(rows):
    return lax.broadcasted_iota(jnp.int32, (rows, 128), 1) < HEAD_DIM


def pair(a, b):
    return jnp.concatenate([a, b], axis=1)


def fold(x, lo):
    cols = slice(lo, lo + HEAD_DIM)
    return pair(x[: ROWS // 2, cols], x[ROWS // 2 :, cols])


def probabilities(qd, kv):
    left = left_half(ROWS)
    scores = dot(jnp.where(left, qd, jnp.zeros_like(qd)), kv, NT)
    top = jnp.max(scores, axis=1, keepdims=True)
    e = jnp.exp2((scores - top) * EXP2_SCALE)
    inv = 1.0 / jnp.sum(e, axis=1, keepdims=True)
    return e.astype(BF), inv


def both(parts, axis):
    return jnp.concatenate(parts, axis=axis)


def fresh_first(blocks, kv, acc):
    left = left_half(ROWS)
    outs, terms, rows = [], [], []
    for qd in blocks:
        e16, inv = probabilities(qd, kv)
        a16 = (dot(e16, kv) * inv).astype(BF)
        delta = jnp.sum(
            jnp.where(left, 0.0, a16.astype(F32) * qd.astype(F32)), axis=1, keepdims=True
        )
        scaled = (qd.astype(F32) * jnp.where(left, inv * SCALE, inv)).T.astype(BF)
        outs.append((e16, fold(a16, HEAD_DIM), jnp.where(left, inv * SCALE, delta), scaled[:HEAD_DIM]))
        terms.append(e16)
        rows.append(scaled[HEAD_DIM:])
    acc[...] += dot(both(rows, 1), both(terms, 0))
    return outs


def fresh_second(blocks, kv, es, stats, q_scaled, acc):
    left = left_half(ROWS)
    outs, terms = [], []
    for qd, e16, row in zip(blocks, es, stats):
        dprob = dot(jnp.where(left, jnp.zeros_like(qd), qd), kv, NT)
        ds = (e16.astype(F32) * (dprob - row[:, HEAD_DIM : HEAD_DIM + 1])).astype(BF)
        outs.append(fold((dot(ds, kv) * row[:, 0:1]).astype(BF), 0))
        terms.append(ds)
    acc[...] += dot(both(q_scaled, 1), both(terms, 0))
    return outs


def stale_tile(qd, kv):
    e16, inv = probabilities(qd, kv)
    return fold((dot(e16, kv) * inv).astype(BF), HEAD_DIM)


def loop(lo, hi, fn):
    def step(n, carry):
        fn(n)
        return carry

    lax.fori_loop(lo, hi, step, 0)


def kernel(
    x_hbm, s_hbm, wq_hbm, wk_hbm, wv_hbm, wo_hbm, g_hbm,
    mixed_out, gradx_out, gv_out, go_out,
    x2, g2, s, wq, wk, wv, wo, load_sem, share_sem,
    st_kv, st_qd, st_ks,
    kv_w, qd_w, ks_w, kv_q, qd_q, ks_q,
    send_w, recv_w, send_q, recv_q,
    e_w, e_q, stats, q_scaled, acc, kmix,
    out_a, out_dq, out_t, out_dv, out_dk, part_dv, part_dk, row_a, row_dq, row_t,
    home_a, home_dq, home_t, home_dv, home_dk, home_dvp, home_dkp, sib_dv, sib_dk, pair_send, pair_recv,
    hsend, hrecv, psend, precv, asend, arecv, apsend, aprecv,
    x_t, dv2, grads, from_y, ysum, from_xz, gathered, final,
    mixed, gradx, gv, go,
    dsem, ysend, yrecv, xsend, xrecv, gsend, grecv, out_sem,
):
    img = lax.axis_index("img")
    me = lax.axis_index("patch")
    core = lax.rem(img, 2)
    zlo = lax.rem(img // 2, 2)
    yy = img // 4
    mine_e = me // 4
    shared_core = lax.rem(me // 2, 2)
    shared_img = img - core + shared_core
    holds = core == shared_core
    first_q = 4 * lax.rem(me, 2) + 2 * core
    my_helper_core = lax.rem(me, 4) // 2

    def helper(c, e):
        return img - core + my_helper_core, 4 * e + 2 * c + me // 4
    core_one = img - core + 1
    sibling = img + 1 - 2 * core

    loads = [
        pltpu.make_async_copy(src, dst, load_sem.at[n])
        for n, (src, dst) in enumerate(
            (
                (x_hbm, x2.at[core]), (wk_hbm, wk), (wv_hbm, wv), (wq_hbm, wq),
                (g_hbm, g2.at[core]), (wo_hbm, wo), (s_hbm, s),
            )
        )
    ]
    for copy in loads[:3]:
        copy.start()

    barrier = pltpu.get_barrier_semaphore()
    for off in range(1, N_PATCH):
        pl.semaphore_signal(
            barrier, inc=1, device_id=(img, lax.rem(me + off, N_PATCH)), device_id_type=MESH
        )
    for off in range(1, N_IMG):
        pl.semaphore_signal(
            barrier, inc=1, device_id=(lax.rem(img + off, N_IMG), me), device_id_type=MESH
        )
    for off in range(1, N_PATCH):
        for there in (img + 2 - 4 * zlo, sibling):
            pl.semaphore_signal(
                barrier, inc=1, device_id=(there, lax.rem(me + off, N_PATCH)), device_id_type=MESH
            )

    def turn(off, sign=1):
        dx = off % 4 if sign == 1 else 4 - off % 4
        return lax.rem(me // 4 + off // 4, 2) * 4 + lax.rem(me + dx, 4)

    def peers(fn):
        for off in (5, 1, 7, 3, 4, 6, 2):
            fn(turn(off))

    def to_whole(kind, stage, land, peer):
        return pltpu.make_async_remote_copy(
            src_ref=stage.at[peer], dst_ref=land.at[me],
            send_sem=send_w.at[kind, peer], recv_sem=recv_w.at[kind, me],
            device_id=(img, peer), device_id_type=MESH,
        )

    def from_whole(kind, land, peer):
        return pltpu.make_async_remote_copy(
            src_ref=land.at[peer], dst_ref=land.at[peer],
            send_sem=send_w.at[kind, peer], recv_sem=recv_w.at[kind, peer],
            device_id=(img, peer), device_id_type=MESH,
        )

    def to_quarter(kind, stage, land, e, n):
        peer = 4 * e + 2 * core + n
        return peer, pltpu.make_async_remote_copy(
            src_ref=stage.at[N_PATCH + e], dst_ref=land.at[me],
            send_sem=send_q.at[kind, peer], recv_sem=recv_q.at[kind, me],
            device_id=(img, peer), device_id_type=MESH,
        )

    def each_quarter(fn):
        for e in range(2):
            for n in range(2):
                fn(e, n)

    def send_quarter(kind, stage, land):
        def one(e, n):
            peer, copy = to_quarter(kind, stage, land, e, n)

            @pl.when(peer != me)
            def _():
                copy.start()

        each_quarter(one)

        @pl.when(holds)
        def _():
            land[me] = stage[N_PATCH + mine_e]

    def from_quarter(kind, land, peer):
        return pltpu.make_async_remote_copy(
            src_ref=land.at[peer], dst_ref=land.at[peer],
            send_sem=send_q.at[kind, peer], recv_sem=recv_q.at[kind, peer],
            device_id=(img, peer), device_id_type=MESH,
        )

    def hand_over(n, src, dst):
        return pltpu.make_async_remote_copy(
            src_ref=src, dst_ref=dst, send_sem=pair_send.at[n], recv_sem=pair_recv.at[n],
            device_id=(sibling, me), device_id_type=MESH,
        )

    def pass_keys(n, kind, land):
        @pl.when(holds)
        def _():
            peers(lambda peer: from_quarter(kind, land, peer).wait_recv())
            hand_over(n, land, land).start()

    def wait_keys(n, land):
        @pl.when(jnp.logical_not(holds))
        def _():
            hand_over(n, land, land).wait_recv()

    def pass_sums(n, part, arrived):
        @pl.when(jnp.logical_not(holds))
        def _():
            hand_over(n, part, arrived).start()

    def send_sums(n, kind, part, arrived, land):
        @pl.when(holds)
        def _():
            hand_over(n, part, arrived).wait_recv()
            part[...] = (part[...].astype(F32) + arrived[...].astype(F32)).astype(BF)
            peers(lambda peer: go_home(kind, part, land, peer).start())
            land[me] = part[me]

    def receive_sums(kind, land):
        def one(e, n):
            peer = 4 * e + 2 * core + n

            @pl.when(peer != me)
            def _():
                come_home(kind, land, peer).wait_recv()

        each_quarter(one)

    def quarter_rows(e):
        there, peer = helper(core, e)
        here = jnp.logical_and(there == img, peer == me)
        return here, pltpu.make_async_remote_copy(
            src_ref=st_qd.at[N_PATCH + e], dst_ref=qd_q.at[lax.rem(me, 2)],
            send_sem=send_q.at[1, e], recv_sem=recv_q.at[1, lax.rem(me, 2)],
            device_id=(there, peer), device_id_type=MESH,
        )

    def owned(t):
        return jnp.logical_and(holds, first_q + t == me)

    def quarter_rows_in(t):
        return pltpu.make_async_remote_copy(
            src_ref=qd_q.at[t], dst_ref=qd_q.at[t],
            send_sem=send_q.at[1, t], recv_sem=recv_q.at[1, t],
            device_id=(shared_img, first_q + t), device_id_type=MESH,
        )

    def share(core_from, ref, n):
        return pltpu.make_async_remote_copy(
            src_ref=ref.at[core_from], dst_ref=ref.at[core_from],
            send_sem=share_sem.at[n], recv_sem=share_sem.at[2 + n],
            device_id=(sibling, me), device_id_type=MESH,
        )

    def stage_pairs(stage, a, b):
        for h in range(HEADS):
            cols = slice(h * HEAD_DIM, (h + 1) * HEAD_DIM)
            stage[h] = pair(a[:, cols], b[:, cols])

    loads[0].wait()
    loads[1].wait()
    for copy in loads[3:]:
        copy.start()
    key = dot(x2[core], wk[...]).astype(BF)
    loads[2].wait()
    value = dot(x2[core], wv[...]).astype(BF)
    stage_pairs(st_kv, key, value)
    pl.semaphore_wait(barrier, 3 * (N_PATCH - 1) + N_IMG - 1)
    peers(lambda peer: to_whole(0, st_kv, kv_w, peer).start())
    kv_w[me] = st_kv[me]
    loads[3].wait()
    query = dot(x2[core], wq[...]).astype(BF)
    loads[4].wait()
    loads[5].wait()
    dattend = dot(g2[core], wo[...], NT).astype(BF)
    stage_pairs(st_qd, query, dattend)
    for off in range(1, N_PATCH):
        to_whole(1, st_qd, qd_w, turn(off, -1)).start()
    qd_w[me] = st_qd[me]
    send_quarter(0, st_kv, kv_q)
    for e in range(2):
        here, copy = quarter_rows(e)

        @pl.when(jnp.logical_not(here))
        def _():
            copy.start()

        @pl.when(here)
        def _():
            qd_q[lax.rem(me, 2)] = st_qd[N_PATCH + e]

    @pl.when(core == 1)
    def _():
        share(1, x2, 0).start()

    @pl.when(core == 0)
    def _():
        share(0, g2, 1).start()

    loads[6].wait()
    key_old = dot(s[...], wk[...]).astype(BF)
    value_old = dot(s[...], wv[...]).astype(BF)
    stage_pairs(st_ks, key_old, value_old)
    ks_w[me] = st_ks[me]

    @pl.when(core == 0)
    def _():
        share(1, x2, 0).wait_recv()
        x_t[:, :ROWS] = x2[0].T
        x_t[:, ROWS:] = x2[1].T

    @pl.when(core == 1)
    def _():
        share(0, g2, 1).wait_recv()

    def go_home(kind, src, land, peer):
        return pltpu.make_async_remote_copy(
            src_ref=src.at[peer], dst_ref=land.at[me],
            send_sem=hsend.at[kind, peer], recv_sem=hrecv.at[kind, me],
            device_id=(img, peer), device_id_type=MESH,
        )

    def come_home(kind, land, peer):
        return pltpu.make_async_remote_copy(
            src_ref=land.at[peer], dst_ref=land.at[peer],
            send_sem=hsend.at[kind, peer], recv_sem=hrecv.at[kind, peer],
            device_id=(img, peer), device_id_type=MESH,
        )

    def go_home_rows(kind, src, land, t):
        return pltpu.make_async_remote_copy(
            src_ref=src.at[t], dst_ref=land.at[N_PATCH + mine_e],
            send_sem=psend.at[kind, t], recv_sem=precv.at[kind, mine_e],
            device_id=(shared_img, first_q + t), device_id_type=MESH,
        )

    def come_home_rows(kind, land, e):
        there, peer = helper(core, e)
        here = jnp.logical_and(there == img, peer == me)
        return here, pltpu.make_async_remote_copy(
            src_ref=land.at[N_PATCH + e], dst_ref=land.at[N_PATCH + e],
            send_sem=psend.at[kind, e], recv_sem=precv.at[kind, e],
            device_id=(there, peer), device_id_type=MESH,
        )

    def a_home(i):
        return pltpu.make_async_remote_copy(
            src_ref=out_a.at[i], dst_ref=home_a.at[core, me],
            send_sem=asend.at[i], recv_sem=arecv.at[core, me],
            device_id=(core_one, i), device_id_type=MESH,
        )

    def a_in(c, peer):
        return pltpu.make_async_remote_copy(
            src_ref=home_a.at[c, peer], dst_ref=home_a.at[c, peer],
            send_sem=asend.at[peer], recv_sem=arecv.at[c, peer],
            device_id=(core_one, peer), device_id_type=MESH,
        )

    def a_home_rows(t):
        return pltpu.make_async_remote_copy(
            src_ref=row_a.at[t], dst_ref=home_a.at[shared_core, N_PATCH + mine_e],
            send_sem=apsend.at[t], recv_sem=aprecv.at[shared_core, mine_e],
            device_id=(core_one, first_q + t), device_id_type=MESH,
        )

    def a_in_rows(c, e):
        return pltpu.make_async_remote_copy(
            src_ref=home_a.at[c, N_PATCH + e], dst_ref=home_a.at[c, N_PATCH + e],
            send_sem=apsend.at[e], recv_sem=aprecv.at[c, e],
            device_id=helper(c, e), device_id_type=MESH,
        )

    def stays(peer):
        return jnp.logical_and(peer == me, core == 1)

    def put(out):
        for j in range(N_PATCH):
            out[j] = fold(acc[:, j * ROWS : (j + 1) * ROWS].T.astype(BF), 0)

    def clear():
        acc[...] = jnp.zeros_like(acc)

    peers(lambda peer: from_whole(0, kv_w, peer).wait_recv())
    clear()

    def first_pair(i, qd, kv, e, a):
        outs = fresh_first([qd[n] for n in i[0]], kv[...].reshape(TOKENS, 128), acc)
        for n, at, out in zip(*i, outs):
            e[n], a[n], stats[at], q_scaled[at] = out

    def two(k):
        return turn(2 * k), turn(2 * k + 1)

    def first_whole(k):
        i = two(k)

        @pl.when(k == 3)
        def _():
            pass_keys(0, 0, kv_q)

        for n in i:
            @pl.when(n != me)
            def _():
                from_whole(1, qd_w, n).wait_recv()

        first_pair((i, i), qd_w, kv_w, e_w, out_a)
        for n in i:
            @pl.when(jnp.logical_not(stays(n)))
            def _():
                a_home(n).start()

    loop(0, 4, first_whole)

    @pl.when(core == 1)
    def _():
        home_a[1, me] = out_a[me]

    put(out_dv)
    peers(lambda peer: go_home(3, out_dv, home_dv, peer).start())
    home_dv[me] = out_dv[me]

    wait_keys(0, kv_q)
    for t in range(2):
        @pl.when(jnp.logical_not(owned(t)))
        def _():
            quarter_rows_in(t).wait_recv()

    clear()

    first_pair(((0, 1), (N_PATCH, N_PATCH + 1)), qd_q, kv_q, e_q, row_a)
    for t in range(2):
        here = stays(first_q + t)

        @pl.when(jnp.logical_not(here))
        def _():
            a_home_rows(t).start()

        @pl.when(here)
        def _():
            home_a[shared_core, N_PATCH + mine_e] = row_a[t]

    put(part_dv)
    pass_sums(2, part_dv, sib_dv)
    send_sums(2, 5, part_dv, sib_dv, home_dvp)
    peers(lambda peer: to_whole(2, st_ks, ks_w, peer).start())
    send_quarter(2, st_ks, ks_q)

    def unfold(src, r):
        cols = slice(r * HEAD_DIM, (r + 1) * HEAD_DIM)
        return jnp.concatenate([src[h][:, cols] for h in range(HEADS)], axis=1)

    def add_shared(land, parts):
        for e in range(2):
            first = 4 * e + 2 * core
            total = parts[first].astype(F32) + parts[first + 1].astype(F32)
            land[N_PATCH + e] = total.astype(BF)

    def y_copy(off):
        peer = lax.rem(yy + off, 4)
        return pltpu.make_async_remote_copy(
            src_ref=grads.at[:, pl.ds(pl.multiple_of(SLOT * peer, 16), SLOT)],
            dst_ref=from_y.at[off - 1],
            send_sem=ysend.at[off - 1], recv_sem=yrecv.at[off - 1],
            device_id=(4 * peer + 2 * zlo + core, me), device_id_type=MESH,
        )

    grads[:, 800:] = jnp.zeros((N_PATCH, PART - 800, 128), BF)

    def make_grad_out():
        @pl.when(core == 1)
        def _():
            for c in range(2):
                for n in range(N_PATCH):
                    if c == 1:
                        @pl.when(n != me)
                        def _():
                            a_in(c, n).wait_recv()
                    else:
                        a_in(c, n).wait_recv()
                for e in range(2):
                    there, peer = helper(c, e)

                    @pl.when(jnp.logical_not(jnp.logical_and(there == img, peer == me)))
                    def _():
                        a_in_rows(c, e).wait_recv()
            a_t = jnp.concatenate(
                [unfold(home_a.at[c], r).T for c in range(2) for r in range(2)], axis=1
            )
            g_all = g2[...].reshape(2 * ROWS, C)
            for q in range(N_PATCH):
                part = dot(a_t[80 * q : 80 * q + 80], g_all).astype(BF)
                for c in range(10):
                    grads[q, 80 * c : 80 * c + 80] = part[:, 128 * c : 128 * c + 128]
            for off in range(1, 4):
                y_copy(off).start()

    dv_share = pltpu.make_async_remote_copy(
        src_ref=dv2.at[1], dst_ref=dv2.at[1], send_sem=dsem.at[0], recv_sem=dsem.at[1],
        device_id=(sibling, me), device_id_type=MESH,
    )

    def make_grad_value():

        peers(lambda peer: come_home(3, home_dv, peer).wait_recv())
        receive_sums(5, home_dvp)
        add_shared(home_dv, home_dvp)
        for r in range(2):
            dv2[core, r * ROWS // 2 : (r + 1) * ROWS // 2] = unfold(home_dv, r)
        @pl.when(core == 1)
        def _():
            dv_share.start()

        @pl.when(core == 0)
        def _():
            dv_share.wait_recv()
            dv_all = dv2[...].reshape(2 * ROWS, INNER)
            for q in range(N_PATCH):
                part = dot(x_t[160 * q : 160 * q + 160], dv_all).astype(BF)
                for c in range(5):
                    grads[q, 160 * c : 160 * c + 160] = part[:, 128 * c : 128 * c + 128]
            for off in range(1, 4):
                y_copy(off).start()

    clear()

    def second_pair(i, qd, kv, e, out):
        dqs = fresh_second(
            [qd[n] for n in i[0]], kv[...].reshape(TOKENS, 128), [e[n] for n in i[0]],
            [stats[n] for n in i[1]], [q_scaled[n] for n in i[1]], acc,
        )
        for n, dq in zip(i[0], dqs):
            out[n] = dq

    def second_whole(k):
        i = two(k)

        @pl.when(k == 1)
        def _():
            make_grad_out()

        @pl.when(k == 2)
        def _():
            make_grad_value()

        second_pair((i, i), qd_w, kv_w, e_w, out_dq)
        for n in i:
            @pl.when(n != me)
            def _():
                go_home(0, out_dq, home_dq, n).start()

    loop(0, 4, second_whole)
    home_dq[me] = out_dq[me]
    put(out_dk)
    peers(lambda peer: go_home(1, out_dk, home_dk, peer).start())
    home_dk[me] = out_dk[me]

    clear()

    second_pair(((0, 1), (N_PATCH, N_PATCH + 1)), qd_q, kv_q, e_q, row_dq)

    def send_rows(kind, src, land):
        for t in range(2):
            @pl.when(jnp.logical_not(owned(t)))
            def _():
                go_home_rows(kind, src, land, t).start()

            @pl.when(owned(t))
            def _():
                land[N_PATCH + mine_e] = src[t]

    send_rows(0, row_dq, home_dq)
    put(part_dk)
    pass_sums(3, part_dk, sib_dk)

    plane = zlo * N_PATCH + me

    def xz_peer(off):
        there = lax.rem(plane + off, 16)
        return there, there // N_PATCH, lax.rem(there, N_PATCH)

    def xz_send(off):
        there, z_there, p_there = xz_peer(off)
        return pltpu.make_async_remote_copy(
            src_ref=ysum.at[p_there, pl.ds(pl.multiple_of(HALF * z_there, 16), HALF)],
            dst_ref=from_xz.at[plane],
            send_sem=xsend.at[there], recv_sem=xrecv.at[plane],
            device_id=(4 * yy + 2 * z_there + core, p_there), device_id_type=MESH,
        )

    def xz_recv(off):
        there, z_there, p_there = xz_peer(off)
        return pltpu.make_async_remote_copy(
            src_ref=from_xz.at[there], dst_ref=from_xz.at[there],
            send_sem=xsend.at[there], recv_sem=xrecv.at[there],
            device_id=(4 * yy + 2 * z_there + core, p_there), device_id_type=MESH,
        )

    def sum_over_y():
        for off in range(1, 4):
            y_copy(off).wait_recv()

        def y_add(k):
            q = turn(k)
            total = grads[q, pl.ds(pl.multiple_of(SLOT * yy, 16), SLOT)].astype(F32)
            for n in range(3):
                total = total + from_y[n, q].astype(F32)
            ysum[q, :SLOT] = total.astype(BF)
            ysum[q, SLOT:] = jnp.zeros((2 * HALF - SLOT, 128), BF)
            for z_there in range(2):
                there = z_there * N_PATCH + q

                @pl.when(there != plane)
                def _():
                    xz_send(lax.rem(there + 16 - plane, 16)).start()

        loop(0, N_PATCH, y_add)
        from_xz[plane] = ysum[me, pl.ds(pl.multiple_of(HALF * zlo, 16), HALF)]

    peers(lambda peer: from_whole(2, ks_w, peer).wait_recv())
    kmix[0] = ks_w[...]
    kmix[1] = ks_w[...]

    def stale_pair(at, i, qd, kv, ks, out):
        for t in range(2):
            kmix[t, i[t]] = kv[i[t]]
        outs = [stale_tile(qd[at[t]], kmix[t].reshape(TOKENS, 128)) for t in range(2)]
        for t in range(2):
            out[at[t]] = outs[t]
            kmix[t, i[t]] = ks[i[t]]

    def stale_whole(k):
        i = two(k)

        @pl.when(k == 4)
        def _():
            sum_over_y()

        @pl.when(k == 1)
        def _():
            send_sums(3, 4, part_dk, sib_dk, home_dkp)

        @pl.when(k == 3)
        def _():
            pass_keys(1, 2, ks_q)

        stale_pair(i, i, qd_w, kv_w, ks_w, out_t)
        for n in i:
            @pl.when(n != me)
            def _():
                go_home(2, out_t, home_t, n).start()

    loop(0, 4, stale_whole)
    home_t[me] = out_t[me]
    sum_over_y()
    wait_keys(1, ks_q)
    kmix[0] = ks_q[...]
    kmix[1] = ks_q[...]

    stale_pair((0, 1), (first_q, first_q + 1), qd_q, kv_q, ks_q, row_t)
    send_rows(1, row_t, home_t)

    loop(1, 16, lambda off: xz_recv(off).wait_recv())
    total = from_xz[0].astype(F32)
    for n in range(1, 16):
        total = total + from_xz[n].astype(F32)
    gathered[img] = total.astype(BF)

    def gather_send(off):
        peer = lax.rem(img + off, N_IMG)
        return pltpu.make_async_remote_copy(
            src_ref=gathered.at[img], dst_ref=gathered.at[img],
            send_sem=gsend.at[peer], recv_sem=grecv.at[img],
            device_id=(peer, me), device_id_type=MESH,
        )

    def gather_recv(off):
        peer = lax.rem(img + off, N_IMG)
        return pltpu.make_async_remote_copy(
            src_ref=gathered.at[peer], dst_ref=gathered.at[peer],
            send_sem=gsend.at[peer], recv_sem=grecv.at[peer],
            device_id=(peer, me), device_id_type=MESH,
        )

    loop(1, N_IMG, lambda off: gather_send(off).start())

    def receive_rows(kind, land):
        for e in range(2):
            here, copy = come_home_rows(kind, land, e)

            @pl.when(jnp.logical_not(here))
            def _():
                copy.wait_recv()

    peers(lambda peer: come_home(0, home_dq, peer).wait_recv())
    receive_rows(0, home_dq)
    peers(lambda peer: come_home(1, home_dk, peer).wait_recv())
    receive_sums(4, home_dkp)
    add_shared(home_dk, home_dkp)
    dquery = jnp.concatenate([unfold(home_dq, 0), unfold(home_dq, 1)], axis=0)
    dkey = jnp.concatenate([unfold(home_dk, 0), unfold(home_dk, 1)], axis=0)
    gradx[...] = (
        dot(dquery, wq[...], NT) + dot(dkey, wk[...], NT) + dot(dv2[core], wv[...], NT)
    ).astype(BF)
    gradx_copy = pltpu.make_async_copy(gradx, gradx_out.at[0], out_sem.at[0])
    gradx_copy.start()

    peers(lambda peer: come_home(2, home_t, peer).wait_recv())
    receive_rows(1, home_t)
    for r in range(2):
        mixed[r * ROWS // 2 : (r + 1) * ROWS // 2] = dot(unfold(home_t, r), wo[...]).astype(BF)
    mixed_copy = pltpu.make_async_copy(mixed, mixed_out.at[0], out_sem.at[1])
    mixed_copy.start()

    loop(1, N_IMG, lambda off: gather_recv(off).wait_recv())
    for kind in range(2):
        for n in range(4):
            final[kind, SLOT * n : SLOT * n + HALF] = gathered[4 * n + kind].astype(F32)
            final[kind, SLOT * n + HALF : SLOT * (n + 1)] = gathered[4 * n + 2 + kind][
                : SLOT - HALF
            ].astype(F32)
    for c in range(5):
        gv[:, 128 * c : 128 * c + 128] = final[0, 160 * c : 160 * c + 160]
    for c in range(10):
        go[:, 128 * c : 128 * c + 128] = final[1, 80 * c : 80 * c + 80]
    gv_copy = pltpu.make_async_copy(gv, gv_out, out_sem.at[2])
    go_copy = pltpu.make_async_copy(go, go_out, out_sem.at[3])
    gv_copy.start()
    go_copy.start()

    for kind, stage, land in ((0, st_kv, kv_w), (1, st_qd, qd_w), (2, st_ks, ks_w)):
        peers(lambda peer: to_whole(kind, stage, land, peer).wait_send())
    for kind, stage, land in ((0, st_kv, kv_q), (2, st_ks, ks_q)):
        def sent(e, n):
            peer, copy = to_quarter(kind, stage, land, e, n)

            @pl.when(peer != me)
            def _():
                copy.wait_send()

        each_quarter(sent)

    for e in range(2):
        here, copy = quarter_rows(e)

        @pl.when(jnp.logical_not(here))
        def _():
            copy.wait_send()

    @pl.when(holds)
    def _():
        hand_over(0, kv_q, kv_q).wait_send()
        hand_over(1, ks_q, ks_q).wait_send()
        peers(lambda peer: go_home(4, part_dk, home_dkp, peer).wait_send())
        peers(lambda peer: go_home(5, part_dv, home_dvp, peer).wait_send())

    @pl.when(jnp.logical_not(holds))
    def _():
        hand_over(2, part_dv, sib_dv).wait_send()
        hand_over(3, part_dk, sib_dk).wait_send()

    @pl.when(core == 1)
    def _():
        share(1, x2, 0).wait_send()
        dv_share.wait_send()

    @pl.when(core == 0)
    def _():
        share(0, g2, 1).wait_send()

    for kind, src, land in (
        (0, out_dq, home_dq), (1, out_dk, home_dk), (2, out_t, home_t),
        (3, out_dv, home_dv),
    ):
        peers(lambda peer: go_home(kind, src, land, peer).wait_send())
    for kind, src, land in ((0, row_dq, home_dq), (1, row_t, home_t)):
        for t in range(2):
            @pl.when(jnp.logical_not(owned(t)))
            def _():
                go_home_rows(kind, src, land, t).wait_send()

    for n in range(N_PATCH):
        @pl.when(jnp.logical_not(stays(n)))
        def _():
            a_home(n).wait_send()

    for t in range(2):
        @pl.when(jnp.logical_not(stays(first_q + t)))
        def _():
            a_home_rows(t).wait_send()

    for off in range(1, 4):
        y_copy(off).wait_send()
    loop(1, 16, lambda off: xz_send(off).wait_send())
    loop(1, N_IMG, lambda off: gather_send(off).wait_send())
    for copy in (gradx_copy, mixed_copy, gv_copy, go_copy):
        copy.wait()


def pass_on(*refs):
    sources, results, held = refs[:4], refs[4:8], refs[8:12]
    load_sem, store_sem = refs[12:]
    loads = [pltpu.make_async_copy(sources[n], held[n], load_sem.at[n]) for n in range(4)]
    stores = [pltpu.make_async_copy(held[n], results[n], store_sem.at[n]) for n in range(4)]
    for copy in loads:
        copy.start()
    for load, store in zip(loads, stores):
        load.wait()
        store.start()
    for store in stores:
        store.wait()


def vm(*shape, dtype=BF):
    return pltpu.VMEM(shape, dtype)


def dma(*shape):
    return pltpu.SemaphoreType.DMA(shape)


def on_device(latents_now, latents_stale, w_query, w_key, w_value, w_out, cotangent):
    half = ROWS // 2
    shapes = (
        jax.ShapeDtypeStruct((1, ROWS, C), BF),
        jax.ShapeDtypeStruct((1, ROWS, C), BF),
        jax.ShapeDtypeStruct((C // N_PATCH, INNER), F32),
        jax.ShapeDtypeStruct((INNER // N_PATCH, C), F32),
    )
    anywhere = pl.BlockSpec(memory_space=pl.ANY)
    results = pl.pallas_call(
        kernel,
        out_shape=shapes,
        in_specs=[anywhere] * 7,
        out_specs=[anywhere] * 4,
        scratch_shapes=[
            vm(2, ROWS, C), vm(2, ROWS, C), vm(ROWS, C), vm(C, INNER), vm(C, INNER), vm(C, INNER), vm(INNER, C),
            dma(7), dma(4),
            vm(10, ROWS, 128), vm(10, ROWS, 128), vm(10, ROWS, 128),
            vm(8, ROWS, 128), vm(8, ROWS, 128), vm(8, ROWS, 128),
            vm(8, ROWS, 128), vm(2, ROWS, 128), vm(8, ROWS, 128),
            dma(3, 8), dma(3, 8), dma(3, 8), dma(3, 8),
            vm(8, ROWS, TOKENS), vm(2, ROWS, TOKENS), vm(10, ROWS, 128, dtype=F32), vm(10, HEAD_DIM, ROWS),
            vm(HEAD_DIM, TOKENS, dtype=F32), vm(2, 8, ROWS, 128),
            vm(8, half, 128), vm(8, half, 128), vm(8, half, 128), vm(8, half, 128), vm(8, half, 128),
            vm(8, half, 128), vm(8, half, 128), vm(2, half, 128), vm(2, half, 128), vm(2, half, 128),
            vm(2, 10, half, 128), vm(10, half, 128), vm(10, half, 128), vm(10, half, 128), vm(10, half, 128),
            vm(8, half, 128), vm(8, half, 128), vm(8, half, 128), vm(8, half, 128), dma(4), dma(4),
            dma(6, 8), dma(6, 8), dma(2, 2), dma(2, 2), dma(8), dma(2, 8), dma(2), dma(2, 2),
            vm(C, 2 * ROWS), vm(2, ROWS, INNER), vm(8, PART, 128), vm(3, 8, SLOT, 128), vm(8, 2 * HALF, 128),
            vm(16, HALF, 128), vm(16, HALF, 128), vm(2, PART, 128, dtype=F32),
            vm(ROWS, C), vm(ROWS, C), vm(C // N_PATCH, INNER, dtype=F32), vm(INNER // N_PATCH, C, dtype=F32),
            dma(2), dma(3), dma(3), dma(16), dma(16), dma(16), dma(16), dma(4),
        ],
        compiler_params=pltpu.CompilerParams(
            collective_id=0, has_side_effects=True, vmem_limit_bytes=56 * 2**20
        ),
        cost_estimate=pl.CostEstimate(flops=10**10, bytes_accessed=12 * 2**20, transcendentals=10**7),
    )(latents_now[0], latents_stale[0], w_query, w_key, w_value, w_out, cotangent[0])
    return pl.pallas_call(
        pass_on,
        out_shape=shapes,
        in_specs=[anywhere] * 4,
        out_specs=[anywhere] * 4,
        scratch_shapes=[pltpu.VMEM(shape.shape, shape.dtype) for shape in shapes] + [dma(4), dma(4)],
        compiler_params=pltpu.CompilerParams(vmem_limit_bytes=56 * 2**20),
        cost_estimate=pl.CostEstimate(flops=0, bytes_accessed=2 * 2**20, transcendentals=0),
    )(*results)


def solution(mesh):
    rows = P("img", "patch", None)
    return jax.shard_map(
        on_device,
        mesh=mesh,
        in_specs=(rows, rows, P(), P(), P(), P(), rows),
        out_specs=(rows, rows, P("patch", None), P("patch", None)),
        check_vma=False,
    )
```
